128 devices in a mesh: dp: 2 (over core), row: 8 (over x_lo, y), col: 8 (over z, x_hi).
Axes of the slice: x: 4 (x_hi: 2, x_lo: 2; x = x_hi * 2 + x_lo), y: 4, z: 4, core: 2. Of those that a mesh axis runs over, the one named last changes fastest.
Arguments:
- query: bfloat16 [2, 2, 512, 8192], P('dp', None, None, 'col'), may hold values from -6 to 6
- key: bfloat16 [2, 2, 512, 8192], P('dp', None, None, 'col'), may hold values from -6 to 6
- value: bfloat16 [2, 2, 512, 8192], P('dp', None, None, 'row'), may hold values from -6 to 6
- out_grad: bfloat16 [2, 2, 512, 8192], P('dp', None, None, 'row'), may hold values from -6 to 6
- rate: float32 [2, 2, 512], P('dp'), may hold values from 6.1035156e-05 to 0.00048828125
- memory_init: float32 [8192, 8192], P('row', 'col'), may hold values from -0.0625 to 0.0625
- memory_cot: float32 [8192, 8192], P('row', 'col'), may hold values from -128 to 128
Outputs:
- query_grad: bfloat16 [2, 2, 512, 8192], P('dp', None, 'row', 'col')
- key_grad: bfloat16 [2, 2, 512, 8192], P('dp', None, 'row', 'col')
- value_grad: bfloat16 [2, 2, 512, 8192], P('dp', None, 'col', 'row')
- init_grad: float32 [8192, 8192], P('row', 'col')
The draws below stay inside these ranges and needn't reach their ends.
All inputs are finite; a program needn't handle non-finite values.
Results may differ from the reference program's by a relative error of at most 0.025.
Values may be sent and summed in bfloat16 or wider, within the bound.
A program may use at most 128 MiB of HBM per device.

```python
import math
import jax
import jax.numpy as jnp

D = 8192
BLOCK = 512
BLOCKS = 2
SEQS = 2


def block_levels(own_key, shape, cuts, least, largest):
    gain, own = 1.0, jax.random.fold_in(own_key, 6)
    for dim, blocks in cuts:
        heights = jnp.exp(jax.random.uniform(jax.random.fold_in(own, dim), (blocks,), jnp.float32, least / len(cuts), largest / len(cuts)))
        gain = gain * jnp.repeat(heights, shape[dim] // blocks).reshape([-1 if axis == dim else 1 for axis in range(len(shape))])
    return gain


def gaussian(stream_key, extent, width, limit, pieces=(), held_as=jnp.bfloat16):
    gain = block_levels(stream_key, extent, pieces, -0.22, 0.18) if pieces else 1.0
    result = jax.random.normal(stream_key, extent, jnp.float32) * width * gain
    return jnp.minimum(jnp.maximum(result, -limit), limit).astype(held_as)


def setup_inputs(seed: int = 0) -> dict:
    arg_keys = jax.random.split(jax.random.key(seed), 8)
    return {
        "query": gaussian(arg_keys[0], (SEQS, BLOCKS, BLOCK, D), 1.0, 6.0, ((0, 2), (3, 8))),
        "key": gaussian(arg_keys[1], (SEQS, BLOCKS, BLOCK, D), 1.0, 6.0, ((0, 2), (3, 8))),
        "value": gaussian(arg_keys[2], (SEQS, BLOCKS, BLOCK, D), 1.0, 6.0, ((0, 2), (3, 8))),
        "out_grad": gaussian(arg_keys[3], (SEQS, BLOCKS, BLOCK, D), 1.0, 6.0, ((0, 2), (3, 8))),
        "rate": jnp.clip(jnp.exp(math.log(0.00048828125) - 2.0794415 * jax.random.uniform(arg_keys[4], (SEQS, BLOCKS, BLOCK), jnp.float32) ** block_levels(arg_keys[4], (SEQS, BLOCKS, BLOCK), ((0, 2),), -0.2, 0.2)), 6.103515625e-05, 0.00048828125),
        "memory_init": gaussian(arg_keys[5], (D, D), D ** -0.5, 0.0625, ((0, 8), (1, 8)), jnp.float32),
        "memory_cot": gaussian(arg_keys[6], (D, D), (BLOCK ** 0.5), 128.0, ((0, 8), (1, 8)), jnp.float32),
    }


def reference(query, key, value, out_grad, rate, memory_init, memory_cot):
    query_list, key_list, value_list = [], [], []
    init_grad = jnp.zeros(memory_init.shape, jnp.float32)
    for seq_index in range(SEQS):
        memory = memory_init
        moment = jnp.zeros(memory_init.shape, jnp.float32)
        halves, weights = [], []
        for block_index in range(BLOCKS):
            key_rows = key[seq_index, block_index]
            memory_half = memory.astype(jnp.bfloat16)
            errors = jnp.dot(key_rows, memory_half.T, preferred_element_type=jnp.float32) - value[seq_index, block_index].astype(jnp.float32)
            weighted = (rate[seq_index, block_index][:, None] * errors).astype(jnp.bfloat16)
            step_grad = jnp.dot(weighted.T, key_rows, preferred_element_type=jnp.float32)
            moment = 0.9 * moment - step_grad
            memory = 0.999 * memory + moment
            halves.append(memory_half)
            weights.append(weighted)
        adjoint = memory_cot
        moment_adj = jnp.zeros(memory_init.shape, jnp.float32)
        query_out, key_out, value_out = [None] * BLOCKS, [None] * BLOCKS, [None] * BLOCKS
        for block_index in reversed(range(BLOCKS)):
            key_rows = key[seq_index, block_index]
            grad_rows = out_grad[seq_index, block_index]
            summed_adj = adjoint + moment_adj
            summed_half = summed_adj.astype(jnp.bfloat16)
            err_grad = (-(rate[seq_index, block_index][:, None] * jnp.dot(key_rows, summed_half.T, preferred_element_type=jnp.float32))).astype(jnp.bfloat16)
            value_out[block_index] = -err_grad
            key_out[block_index] = (jnp.dot(err_grad, halves[block_index], preferred_element_type=jnp.float32) - jnp.dot(weights[block_index], summed_half, preferred_element_type=jnp.float32)).astype(jnp.bfloat16)
            query_out[block_index] = jnp.dot(grad_rows, halves[block_index], preferred_element_type=jnp.float32).astype(jnp.bfloat16)
            adjoint = 0.999 * adjoint + jnp.dot(grad_rows.T, query[seq_index, block_index], preferred_element_type=jnp.float32) + jnp.dot(err_grad.T, key_rows, preferred_element_type=jnp.float32)
            moment_adj = 0.9 * summed_adj
        init_grad = init_grad + adjoint
        query_list.append(jnp.stack(query_out))
        key_list.append(jnp.stack(key_out))
        value_list.append(jnp.stack(value_out))
    return (jnp.stack(query_list), jnp.stack(key_list), jnp.stack(value_list), init_grad)
```

```python
import functools

import jax
import jax.numpy as jnp
from jax import lax
from jax.experimental import pallas as pl
from jax.experimental.pallas import tpu as pltpu
from jax.sharding import PartitionSpec as P

MESH = pl.DeviceIdType.MESH
BF, F32 = jnp.bfloat16, jnp.float32
W = 1024
SH = 64
NJ = 4
CW, RW = W // NJ, SH // NJ
ALL = slice(0, W)
X_FIRST = frozenset([(0, 1), (1, 1), (1, 3), (2, 1), (3, 1)])
UNIT_US = 22.3
HOP_US = 1.0
NT = (((1,), (1,)), ((), ()))
TN = (((0,), (0,)), ((), ()))


class Task:
    def __init__(self, name, needs, waits, cost, body, starts, rank):
        self.name, self.needs, self.waits, self.cost = name, needs, waits, cost
        self.body, self.starts, self.rank = body, starts, rank


def order_tasks(tasks, links, sizes):
    free, arrive, done, now = {}, {}, {}, 0.0
    left, result = list(tasks), []
    while left:
        best = None
        for task in left:
            if any(n not in done for n in task.needs) or any(w not in arrive for w in task.waits):
                continue
            ready = max([now] + [done[n] for n in task.needs] + [arrive[w] for w in task.waits])
            key = (ready, task.rank)
            if best is None or key < best[0]:
                best = (key, task)
        (ready, _), task = best
        now = ready + task.cost
        done[task.name] = now
        for copy in task.starts:
            link = links[copy]
            begin = max(now, free.get(link, 0.0))
            free[link] = begin + sizes[copy]
            arrive[copy] = free[link] + HOP_US
        left.remove(task)
        result.append(task)
    return result, now


def kernel(
    q_hbm, k_hbm, v_hbm, y_hbm, r_ref, m_hbm, c_hbm,
    qg_ref, kg_ref, vg_ref, ig_hbm,
    kb, qb, yb, vb, mf, cf, mh0, mh1, ch, ph0, part, full, rbuf, part2, rbuf2, abf, arec, rc,
    ssem, rsem, lsem,
):
    dp, row, col = lax.axis_index("dp"), lax.axis_index("row"), lax.axis_index("col")
    z, xh = col // 2, col % 2
    xl, y = row // 4, row % 4
    zp, zm, z2, xo = (z + 1) % 4, (z + 3) % 4, (z + 2) % 4, 1 - xh
    yp, ym, y2, lo = (y + 1) % 4, (y + 3) % 4, (y + 2) % 4, 1 - xl
    device = {
        "z+": (dp, row, zp * 2 + xh),
        "z-": (dp, row, zm * 2 + xh),
        "xh": (dp, row, z * 2 + xo),
        "y+": (dp, xl * 4 + yp, col),
        "y-": (dp, xl * 4 + ym, col),
        "xl": (dp, lo * 4 + y, col),
        "dp": (1 - dp, row, col),
    }

    loads = {}

    def load(name, src, dst):
        copy = pltpu.make_async_copy(src, dst, lsem.at[len(loads)])
        copy.start()
        loads[name] = copy

    def rows_of(g):
        return pl.ds(g * CW, CW)

    load("K1", k_hbm.at[0, 1], kb.at[1])
    for g in range(NJ):
        load(("C", g), c_hbm.at[rows_of(g)], cf.at[rows_of(g)])
    load("K0", k_hbm.at[0, 0], kb.at[0])
    for g in range(NJ):
        load(("M", g), m_hbm.at[rows_of(g)], mf.at[rows_of(g)])
    load("V", v_hbm.at[0, :, col], vb)
    load("Y0", y_hbm.at[0, 0], yb.at[0])
    load("Y1", y_hbm.at[0, 1], yb.at[1])
    load("Q1", q_hbm.at[0, 1], qb.at[1])
    load("Q0", q_hbm.at[0, 0], qb.at[0])
    loaded = set()

    def need(*names):
        for name in names:
            if name not in loaded:
                loaded.add(name)
                loads[name].wait()

    barrier = pltpu.get_barrier_semaphore()
    for partner in device.values():
        pl.semaphore_signal(barrier, inc=1, device_id=partner, device_id_type=MESH)

    at = lax.broadcasted_iota(jnp.int32, (SH, 8 * SH), 1)
    own = lax.broadcasted_iota(jnp.int32, (SH, 8 * SH), 0) + col * SH
    for b in range(2):
        picked = jnp.where(at == own, jnp.broadcast_to(r_ref[0, b : b + 1, :], (SH, 8 * SH)), 0.0)
        rc[b] = jnp.broadcast_to(jnp.sum(picked, axis=1, keepdims=True), (SH, 128))

    copies, links, sizes = {}, {}, {}

    def copy(name, link, src, dst, units):
        index = len(copies)
        copies[name] = pltpu.make_async_remote_copy(
            src_ref=src, dst_ref=dst, send_sem=ssem.at[index], recv_sem=rsem.at[index],
            device_id=device[link], device_id_type=MESH,
        )
        links[name] = "x" if link in ("xh", "xl") else link
        sizes[name] = units * (UNIT_US if link != "dp" else 1.2)

    tasks = []

    def task(name, needs, waits, cost, body, starts, rank):
        tasks.append(Task(name, needs, waits, cost, body, starts, rank))

    def f32(ref, *index):
        return ref[index].astype(F32)

    def finish(q, cs, rs, total):
        b = 1 if q in (0, 3) else 0
        wide = total.shape[1]
        rate = jnp.broadcast_to(rc[b, rs, 0:1], total.shape)
        if q in (0, 2):
            scaled = (rate * total).astype(BF)
            vg_ref[0, b, rs, cs] = scaled
            full[q, z, xh, rs, cs] = -scaled
        else:
            full[q, z, xh, rs, cs] = (rate * (total - f32(vb, b, rs, cs))).astype(BF)

    def reduce_job(tag, q, rs, cs, rank, P4, R, first, pieces, names, after, after_cost, after_starts):
        ring, ahead, behind, far, mine, other = pieces
        up, down, side = names
        u = (rs.stop - rs.start) * (cs.stop - cs.start) / (SH * W) / 8.0

        def part_at(i, half):
            return P4(i, half)

        def slot(k):
            return R.at[q, k, rs, cs]

        n = lambda k: (tag, q, rank, k)
        copy(n("D1p"), up, part_at(far, mine), slot(0), u)
        copy(n("D1m"), down, part_at(far, other), slot(1), u)
        copy(n("D2pA"), up, part_at(ahead, mine), slot(2), u)
        copy(n("D2pB"), up, part_at(ahead, other), slot(3), u)
        copy(n("D2mA"), down, part_at(behind, mine), slot(4), u)
        copy(n("D2mB"), down, part_at(behind, other), slot(5), u)
        copy(n("DX"), side, part_at(ring, other), slot(6), u)

        def add(ref, *slots):
            total = ref[...].astype(F32)
            for k in slots:
                total = total + R[q, k, rs, cs].astype(F32)
            return total

        def s1p():
            ref = part_at(ahead, mine)
            ref[...] = add(ref, 0).astype(BF)

        def s1m():
            ref = part_at(behind, other)
            ref[...] = add(ref, 1).astype(BF)

        def s2():
            ref = part_at(ring, other)
            ref[...] = add(ref, 3, 5).astype(BF)

        def s3():
            after(rs, cs, add(part_at(ring, mine), 2, 4, 6))

        vpu = u * 8 * 0.15 + 0.05
        task(n("s1p"), [first], [n("D1p")], vpu, s1p, [n("D2pA")], rank)
        task(n("s1m"), [first], [n("D1m")], vpu, s1m, [n("D2mB")], rank)
        task(n("s2"), [n("s1p"), n("s1m")], [n("D2pB"), n("D2mB")], vpu, s2, [n("DX")], rank)
        task(n("s3"), [n("s2")], [n("D2pA"), n("D2mA"), n("DX")], vpu + after_cost, s3, after_starts, rank)
        return [n("D1p"), n("D1m"), n("D2pB"), n("D2mA")], n("s3")

    def col_z(q, rs, cs, rank, first):
        u = (rs.stop - rs.start) * (cs.stop - cs.start) / (SH * W) / 8.0
        tag = "cz"
        n = lambda k: (tag, q, rank, k)

        def P4(i, half):
            return part.at[q, i, half, rs, cs]

        def F4(i, half):
            return full.at[q, i, half, rs, cs]

        copy(n("GX"), "xh", F4(z, xh), F4(z, xh), u)
        copy(n("Gop"), "z+", F4(z, xh), F4(z, xh), u)
        copy(n("Gom"), "z-", F4(z, xh), F4(z, xh), u)
        copy(n("Gtp"), "z+", F4(z, xo), F4(z, xo), u)
        copy(n("Gtm"), "z-", F4(z, xo), F4(z, xo), u)
        copy(n("Fp"), "z+", F4(zm, xh), F4(zm, xh), u)
        copy(n("Fm"), "z-", F4(zp, xo), F4(zp, xo), u)
        starts, last = reduce_job(
            tag, q, rs, cs, rank, P4, rbuf, first, (z, zp, zm, z2, xh, xo), ("z+", "z-", "xh"),
            lambda rs, cs, total: finish(q, cs, rs, total), 0.1, [n("GX"), n("Gop"), n("Gom")],
        )
        task(n("s4"), [last], [n("GX")], 0.05, None, [n("Gtp"), n("Gtm")], rank)
        task(n("s5p"), [last], [n("Gop")], 0.05, None, [n("Fp")], rank)
        task(n("s5m"), [last], [n("Gtm")], 0.05, None, [n("Fm")], rank)
        task(n("end"), [n("s4"), n("s5p"), n("s5m")], [n("Gom"), n("Gtp"), n("Fp"), n("Fm")], 0.05, None, [], rank)
        return starts, n("end")

    def col_x(q, rs, cs, rank, first):
        u = (rs.stop - rs.start) * (cs.stop - cs.start) / (SH * W) / 8.0
        half = (cs.stop - cs.start) // 2
        cl, cr = slice(cs.start, cs.start + half), slice(cs.start + half, cs.stop)
        n = lambda k: ("cx", q, rank, k)

        def P3(i, c):
            return part.at[q, i, xh, rs, c]

        def F3(i, c):
            return full.at[q, i, xh, rs, c]

        def slot(k, c):
            return rbuf.at[q, k, rs, c]

        copy(n("DX"), "xh", part.at[q, :, xo, rs, cs], rbuf.at[q, pl.ds(0, 4), rs, cs], 4 * u)
        copy(n("D1p"), "z+", P3(z2, cl), slot(4, cl), u / 2)
        copy(n("D1m"), "z-", P3(z2, cr), slot(4, cr), u / 2)
        copy(n("D2pL"), "z+", P3(zp, cl), slot(5, cl), u / 2)
        copy(n("D2pR"), "z+", P3(zp, cr), slot(5, cr), u / 2)
        copy(n("D2mL"), "z-", P3(zm, cl), slot(6, cl), u / 2)
        copy(n("D2mR"), "z-", P3(zm, cr), slot(6, cr), u / 2)
        copy(n("Gp"), "z+", F3(z, cs), F3(z, cs), u)
        copy(n("Gm"), "z-", F3(z, cs), F3(z, cs), u)
        copy(n("Fp"), "z+", F3(zm, cl), F3(zm, cl), u / 2)
        copy(n("Fm"), "z-", F3(zp, cr), F3(zp, cr), u / 2)
        copy(n("X0"), "xh", F3(z, cs), F3(z, cs), u)
        copy(n("Xm"), "xh", F3(zm, cs), F3(zm, cs), u)
        copy(n("Xp"), "xh", F3(zp, cs), F3(zp, cs), u)
        copy(n("X2"), "xh", F3(z2, cs), F3(z2, cs), u)

        def s1():
            for i in range(4):
                part[q, i, xh, rs, cs] = (f32(part, q, i, xh, rs, cs) + f32(rbuf, q, i, rs, cs)).astype(BF)

        def s2p():
            part[q, zp, xh, rs, cl] = (f32(part, q, zp, xh, rs, cl) + f32(rbuf, q, 4, rs, cl)).astype(BF)

        def s2m():
            part[q, zm, xh, rs, cr] = (f32(part, q, zm, xh, rs, cr) + f32(rbuf, q, 4, rs, cr)).astype(BF)

        def s3():
            finish(q, cs, rs, f32(part, q, z, xh, rs, cs) + f32(rbuf, q, 5, rs, cs) + f32(rbuf, q, 6, rs, cs))

        vpu = u * 8 * 0.15 + 0.05
        task(n("s1"), [first], [n("DX")], 2 * vpu, s1, [n("D1p"), n("D1m"), n("D2pR"), n("D2mL")], rank)
        task(n("s2p"), [n("s1")], [n("D1p")], vpu, s2p, [n("D2pL")], rank)
        task(n("s2m"), [n("s1")], [n("D1m")], vpu, s2m, [n("D2mR")], rank)
        task(n("s3"), [n("s2p"), n("s2m")], [n("D2pL"), n("D2pR"), n("D2mL"), n("D2mR")], vpu + 0.1, s3,
             [n("Gp"), n("Gm"), n("X0")], rank)
        task(n("s4p"), [n("s3")], [n("Gp")], 0.05, None, [n("Fp"), n("Xm")], rank)
        task(n("s4m"), [n("s3")], [n("Gm")], 0.05, None, [n("Fm"), n("Xp")], rank)
        task(n("s5"), [n("s4p"), n("s4m")], [n("Fp"), n("Fm")], 0.05, None, [n("X2")], rank)
        task(n("end"), [n("s5")], [n("X0"), n("Xm"), n("Xp"), n("X2")], 0.05, None, [], rank)
        return [n("DX")], n("end")

    def row_job(u, rs, cs, rank, first):
        def P4(i, half):
            return part2.at[u, half, i, rs, cs]

        def store(rs, cs, total):
            ref, b = ((qg_ref, 0), (qg_ref, 1), (kg_ref, 0), (kg_ref, 1))[u]
            ref[0, b, rs, cs] = total.astype(BF)

        return reduce_job(
            "r", u, rs, cs, rank, P4, rbuf2, first, (y, yp, ym, y2, xl, lo), ("y+", "y-", "xl"), store, 0.0, [],
        )

    def dot(a, b, dims=None):
        if dims is None:
            return jnp.dot(a, b, preferred_element_type=F32)
        return lax.dot_general(a, b, dims, preferred_element_type=F32)

    def whole(ref, *index):
        return ref[index].reshape(8 * SH, -1)

    def some(ref, *index):
        return ref[index].reshape(8 * RW, W)

    ends = [[None] * NJ for _ in range(4)]
    everything = slice(0, SH)
    full_cols = slice(0, W)

    def cols(g):
        return slice(g * CW, (g + 1) * CW)

    def toks(k):
        return slice(k * RW, (k + 1) * RW)

    def spread(q, block, width, value, rs, cs):
        part[q, :, :, rs, cs] = value.astype(BF).reshape(4, 2, rs.stop - rs.start, cs.stop - cs.start)

    def phase_a(q, g, rank):
        b, src, half = (1, cf, ch) if q == 0 else (0, mf, mh0)
        rs, cs = everything, cols(g)
        name = ("P", q, g)

        def body():
            need("K1" if q == 0 else "K0", ("C" if q == 0 else "M", g))
            half[cs, :] = src[cs, :].astype(BF)
            spread(q, g, CW, dot(whole(kb, b), half[cs, :], NT), rs, cs)

        make = col_x if (q, g) in X_FIRST else col_z
        starts, ends[q][g] = make(q, rs, cs, rank, name)
        task(name, [], [], 0.45, body, starts, rank)

    for i, (q, g) in enumerate([(0, g) for g in range(NJ)] + [(1, g) for g in range(NJ)]):
        phase_a(q, g, i)

    def project_update(g):
        cs = cols(g)

        def body():
            need("Y1", "Q1", "K1")
            step = dot(full[0, :, :, :, cs].reshape(8 * SH, CW), whole(kb, 1), TN)
            step = step + dot(yb[1, :, :, cs].reshape(8 * SH, CW), whole(qb, 1), TN)
            before = cf[cs, :]
            adjoint = 0.999 * before + step
            cf[cs, :] = adjoint
            ph0[cs, :] = (adjoint + 0.9 * before).astype(BF)

        task(("PU", g), [ends[0][g]], [], 1.0, body, [], 7.5)

    def memory_update(g):
        cs = cols(g)

        def body():
            need("K0")
            step = dot(full[1, :, :, :, cs].reshape(8 * SH, CW), whole(kb, 0), TN)
            mh1[cs, :] = (0.999 * mf[cs, :] - step).astype(BF)

        task(("MU", g), [ends[1][g]], [], 0.6, body, [], 8.5)

    for g in range(NJ):
        project_update(g)
        memory_update(g)
    all_pu = [("PU", g) for g in range(NJ)]
    all_mu = [("MU", g) for g in range(NJ)]

    def query_part(u, g, rank):
        mem = mh0 if u == 0 else mh1
        rs, cs = everything, cols(g)
        name = ("QP", u, g)

        def body():
            need("Y%d" % u)
            value = dot(whole(yb, u), mem[:, cs])
            part2[u, :, :, rs, cs] = value.astype(BF).reshape(2, 4, SH, CW)

        starts, _ = row_job(u, rs, cs, rank, name)
        deps = [("P", 1, g) for g in range(NJ)] if u == 0 else all_mu
        task(name, deps, [], 0.4, body, starts, rank)

    for g in range(NJ):
        query_part(0, g, 20 + g)
        query_part(1, g, 24 + g)

    def phase_b(q, k, rank):
        b, half, deps = (0, ph0, all_pu) if q == 2 else (1, mh1, all_mu)
        rs, cs = toks(k), full_cols
        name = ("P", q, k)

        def body():
            need("K%d" % b)
            lhs = some(kb, b, slice(None), rs)
            for n in range(NJ):
                spread(q, n, CW, dot(lhs, half[cols(n), :], NT), rs, cols(n))

        make = col_x if (q, k) in X_FIRST else col_z
        starts, ends[q][k] = make(q, rs, cs, rank, name)
        task(name, deps, [], 0.7, body, starts, rank)

    for i, (q, k) in enumerate([(2, k) for k in range(NJ)] + [(3, k) for k in range(NJ)]):
        phase_b(q, k, 8 + i)

    def key_part(u, k, rank):
        rs = toks(k)
        f, w, mem, proj = (2, 1, mh0, ph0) if u == 2 else (0, 3, mh1, ch)
        name = ("KP", u, k)

        def body():
            err, wgt = some(full, f, slice(None), slice(None), rs), some(full, w, slice(None), slice(None), rs)
            for n in range(NJ):
                value = dot(err, mem[:, cols(n)]) - dot(wgt, proj[:, cols(n)])
                part2[u, :, :, rs, cols(n)] = value.astype(BF).reshape(2, 4, RW, CW)

        starts, _ = row_job(u, rs, full_cols, rank, name)
        deps = [ends[2][k]] + all_pu + all_mu if u == 2 else [ends[3][k]] + all_pu + all_mu
        task(name, deps, [], 1.2, body, starts, rank)

    for k in range(NJ):
        key_part(2, k, 17 + k / 10)
        key_part(3, k, 18 + k / 10)

    outs = []

    def adjoint_early(g):
        cs = cols(g)

        def body():
            need("Y0", "Q0")
            cf[cs, :] = 0.999 * cf[cs, :] + dot(yb[0, :, :, cs].reshape(8 * SH, CW), whole(qb, 0), TN)

        task(("AE", g), [("PU", g)], [], 0.6, body, [], 30)

    def adjoint_late(g):
        cs = cols(g)

        def body():
            step = dot(full[2, :, :, :, cs].reshape(8 * SH, CW), whole(kb, 0), TN)
            abf[cs, :] = (cf[cs, :] + step).astype(BF)

        copy(("A", g), "dp", abf.at[rows_of(g)], arec.at[rows_of(g)], 0.5)
        task(("AL", g), [("AE", g)] + ends[2], [], 0.6, body, [("A", g)], 19)

        def total():
            cf[cs, :] = abf[cs, :].astype(F32) + arec[cs, :].astype(F32)
            out = pltpu.make_async_copy(cf.at[rows_of(g)], ig_hbm.at[rows_of(g)], lsem.at[len(loads) + g])
            out.start()
            outs.append(out)

        task(("AT", g), [("AL", g)], [("A", g)], 0.3, total, [], 31)

    for g in range(NJ):
        adjoint_early(g)
    for g in range(NJ):
        adjoint_late(g)

    order, _ = order_tasks(tasks, links, sizes)
    pl.semaphore_wait(barrier, len(device))
    need("V")
    for item in order:
        for name in item.waits:
            copies[name].wait_recv()
        if item.body is not None:
            item.body()
        for name in item.starts:
            copies[name].start()
    for name in copies:
        copies[name].wait_send()
    for out in outs:
        out.wait()


def on_device(query, key, value, out_grad, rate, memory_init, memory_cot):
    shared = (1, 2, 8, SH, W)
    vm = pltpu.VMEM
    n_copies = 16 * 15 + 16 * 7 + NJ
    outs = pl.pallas_call(
        kernel,
        out_shape=(
            jax.ShapeDtypeStruct((1, 2, SH, W), BF),
            jax.ShapeDtypeStruct((1, 2, SH, W), BF),
            jax.ShapeDtypeStruct((1, 2, SH, W), BF),
            jax.ShapeDtypeStruct((W, W), F32),
        ),
        in_specs=[pl.BlockSpec(memory_space=pl.ANY)] * 4
        + [pl.BlockSpec(memory_space=vm)]
        + [pl.BlockSpec(memory_space=pl.ANY)] * 2,
        out_specs=(
            pl.BlockSpec(memory_space=vm),
            pl.BlockSpec(memory_space=vm),
            pl.BlockSpec(memory_space=vm),
            pl.BlockSpec(memory_space=pl.ANY),
        ),
        scratch_shapes=[
            vm((2, 8, SH, W), BF),
            vm((2, 8, SH, W), BF),
            vm((2, 8, SH, W), BF),
            vm((2, SH, W), BF),
            vm((W, W), F32),
            vm((W, W), F32),
            vm((W, W), BF),
            vm((W, W), BF),
            vm((W, W), BF),
            vm((W, W), BF),
            vm((4, 4, 2, SH, W), BF),
            vm((4, 4, 2, SH, W), BF),
            vm((4, 7, SH, W), BF),
            vm((4, 2, 4, SH, W), BF),
            vm((4, 7, SH, W), BF),
            vm((W, W), BF),
            vm((W, W), BF),
            vm((2, SH, 128), F32),
            pltpu.SemaphoreType.DMA((n_copies,)),
            pltpu.SemaphoreType.DMA((n_copies,)),
            pltpu.SemaphoreType.DMA((32,)),
        ],
        compiler_params=pltpu.CompilerParams(
            collective_id=0, has_side_effects=True, vmem_limit_bytes=62 * 2**20
        ),
        name="memory_backward",
    )(
        query.reshape(shared), key.reshape(shared), value.reshape(shared), out_grad.reshape(shared), rate,
        memory_init, memory_cot,
    )
    return outs


def solution(mesh):
    placed = (
        P("dp", None, None, "col"),
        P("dp", None, None, "col"),
        P("dp", None, None, "row"),
        P("dp", None, None, "row"),
        P("dp", None, None),
        P("row", "col"),
        P("row", "col"),
    )
    return jax.shard_map(
        on_device,
        mesh=mesh,
        in_specs=placed,
        out_specs=(
            P("dp", None, "row", "col"),
            P("dp", None, "row", "col"),
            P("dp", None, "col", "row"),
            P("row", "col"),
        ),
        check_vma=False,
    )
```

```python
import functools

import jax
import jax.numpy as jnp
from jax import lax
from jax.experimental import pallas as pl
from jax.experimental.pallas import tpu as pltpu
from jax.sharding import PartitionSpec as P

MESH = pl.DeviceIdType.MESH
BF, F32 = jnp.bfloat16, jnp.float32
W = 1024
SH = 64
NJ = 4
NQ = 2
CW, RW = W // NJ, SH // NJ
ALL = slice(0, W)
X_FIRST = frozenset([(0, 1), (0, 3), (1, 1), (1, 3), (3, 1), (3, 2)])
UNIT_US = 22.3
HOP_US = {"z+": 2.3, "z-": 2.3, "y+": 2.3, "y-": 2.3, "x": 3.3, "dp": 1.1}
CORE = 1.0
NT = (((1,), (1,)), ((), ()))
TN = (((0,), (0,)), ((), ()))
ORDER = (
    7, 31, 71, 47, 55, 63, 39, 87, 72, 95, 0, 147, 64, 15, 77, 48, 23, 82, 24, 139, 32, 92, 1, 163,
    140, 40, 65, 49, 16, 93, 56, 25, 103, 132, 8, 33, 2, 141, 41, 17, 57, 100, 26, 156, 66, 133, 9, 50,
    4, 42, 94, 58, 34, 27, 28, 101, 157, 68, 3, 10, 52, 171, 18, 44, 67, 60, 43, 59, 51, 36, 29, 5,
    69, 12, 35, 11, 123, 164, 70, 102, 53, 20, 45, 6, 61, 73, 115, 37, 19, 155, 131, 75, 204, 54, 86, 30,
    90, 88, 207, 84, 165, 116, 13, 108, 38, 76, 74, 21, 46, 81, 79, 62, 89, 142, 158, 91, 99, 124, 117, 107,
    109, 148, 22, 83, 166, 85, 144, 14, 78, 134, 159, 80, 143, 205, 125, 160, 96, 149, 206, 118, 168, 110, 167, 136,
    145, 104, 135, 161, 150, 126, 120, 169, 97, 119, 112, 146, 179, 137, 111, 162, 195, 152, 105, 151, 127, 170, 203, 128,
    121, 176, 138, 98, 199, 113, 192, 129, 153, 200, 122, 183, 106, 177, 114, 175, 130, 212, 210, 214, 191, 154, 201, 187,
    180, 193, 208, 211, 215, 213, 172, 178, 196, 188, 209, 202, 184, 194, 181, 173, 197, 189, 185, 182, 174, 198, 190, 186,
)


class Task:
    def __init__(self, name, needs, groups, waits, cost, body, starts, rank):
        self.name, self.needs, self.groups, self.waits, self.cost = name, needs, groups, waits, cost
        self.body, self.starts, self.rank = body, starts, rank


def order_tasks(tasks, links, sizes):
    free, arrive, done, now = {}, {}, {}, 0.0
    left, result = list(tasks), []
    while left:
        best = None
        for task in left:
            if any(n not in done for n in task.needs) or any(w not in arrive for w in task.waits):
                continue
            ready = max([now] + [done[n] for n in task.needs] + [arrive[w] for w in task.waits])
            key = (ready, task.rank)
            if best is None or key < best[0]:
                best = (key, task)
        (ready, _), task = best
        now = ready + CORE * task.cost + 0.03 * len(task.starts)
        done[task.name] = now
        for copy in task.starts:
            link = links[copy]
            begin = max(now, free.get(link, 0.0))
            free[link] = begin + sizes[copy]
            arrive[copy] = free[link] + HOP_US[link]
        left.remove(task)
        result.append(task)
    return result, now


def kernel(
    q_hbm, k_hbm, v_hbm, y_hbm, r_hbm, m_hbm, c_hbm,
    qg_hbm, kg_hbm, vg_hbm, ig_hbm,
    qg_ref, kg_ref, vg_ref, cf, kb, qb, yb, vb, rb, mf, mh0, mh1, ch, ph0, part, full, rbuf, part2, rbuf2, arec, rc, gpart, gfull, gbuf, fix,
    ssem, rsem, lsem, osem,
):
    dp, row, col = lax.axis_index("dp"), lax.axis_index("row"), lax.axis_index("col")
    z, xh = col // 2, col % 2
    xl, y = row // 4, row % 4
    zp, zm, z2, xo = (z + 1) % 4, (z + 3) % 4, (z + 2) % 4, 1 - xh
    yp, ym, y2, lo = (y + 1) % 4, (y + 3) % 4, (y + 2) % 4, 1 - xl
    device = {
        "z+": (dp, row, zp * 2 + xh),
        "z-": (dp, row, zm * 2 + xh),
        "xh": (dp, row, z * 2 + xo),
        "y+": (dp, xl * 4 + yp, col),
        "y-": (dp, xl * 4 + ym, col),
        "xl": (dp, lo * 4 + y, col),
        "dp": (1 - dp, row, col),
    }

    loads = {}

    def load(name, src, dst):
        copy = pltpu.make_async_copy(src, dst, lsem.at[len(loads)])
        copy.start()
        loads[name] = copy

    def rows_of(g):
        return pl.ds(g * CW, CW)

    load("K1", k_hbm.at[0, 1], kb.at[1])
    for g in range(NJ):
        load(("C", g), c_hbm.at[rows_of(g)], cf.at[rows_of(g)])
    load("K0", k_hbm.at[0, 0], kb.at[0])
    for g in range(NJ):
        load(("M", g), m_hbm.at[rows_of(g)], mf.at[rows_of(g)])
    load("Y1", y_hbm.at[0, 1], yb.at[1])
    load("Q1", q_hbm.at[0, 1], qb.at[1])
    load("R", r_hbm, rb)
    load("V", v_hbm.at[0, :, col], vb)
    load("Y0", y_hbm.at[0, 0], yb.at[0])
    load("Q0", q_hbm.at[0, 0], qb.at[0])
    loaded = set()

    def need(*names):
        for name in names:
            if name not in loaded:
                loaded.add(name)
                loads[name].wait()

    barrier = pltpu.get_barrier_semaphore()
    for partner in device.values():
        pl.semaphore_signal(barrier, inc=1, device_id=partner, device_id_type=MESH)

    def rates():
        need("R")
        at = lax.broadcasted_iota(jnp.int32, (SH, 8 * SH), 1)
        own = lax.broadcasted_iota(jnp.int32, (SH, 8 * SH), 0) + col * SH
        for b in range(2):
            picked = jnp.where(at == own, jnp.broadcast_to(rb[0, b : b + 1, :], (SH, 8 * SH)), 0.0)
            rc[b] = jnp.broadcast_to(jnp.sum(picked, axis=1, keepdims=True), (SH, 128))

    copies, links, sizes, groups, sends = {}, {}, {}, {}, {}

    def waiter(ref, sem):
        return pltpu.make_async_copy(ref, ref, sem)

    def send_group(key, ref):
        sends[key] = waiter(ref, ssem.at[len(sends)]), ssem.at[len(sends)]

    def group(name, ref):
        groups[name] = waiter(ref, rsem.at[len(groups)]), rsem.at[len(groups)]

    def copy(name, link, src, dst, units, job, into=None):
        if into is None:
            group(name, dst)
            into = name
        copies[name] = pltpu.make_async_remote_copy(
            src_ref=src, dst_ref=dst, send_sem=sends[job][1], recv_sem=groups[into][1],
            device_id=device[link], device_id_type=MESH,
        )
        members.setdefault(into, []).append(name)
        links[name] = "x" if link in ("xh", "xl") else link
        sizes[name] = units * (UNIT_US if link != "dp" else 1.2)

    members = {}

    tasks = []

    def task(name, needs, waits, cost, body, starts, rank):
        tasks.append(Task(name, needs, waits, [c for w in waits for c in members[w]], cost, body, starts, rank))

    def out(i, ref, hbm, *index):
        pltpu.make_async_copy(ref.at[index], hbm.at[index], osem.at[i]).start()

    def f32(ref, *index):
        return ref[index].astype(F32)

    def finish(q, cs, rs, total):
        if "V" not in loaded:
            rates()
        need("V")
        b = 1 if q in (0, 3) else 0
        rate = jnp.broadcast_to(rc[b, rs, 0:1], total.shape)
        if q == 2:
            total = total + fix[0, rs, cs]
        if q == 3:
            total = 0.999 * total - fix[1, rs, cs]
        if q in (0, 2):
            scaled = (rate * total).astype(BF)
            vg_ref[0, b, rs, cs] = scaled
            out(2, vg_ref, vg_hbm, 0, b, rs, cs)
            full[q, z, xh, rs, cs] = -scaled
        else:
            full[q, z, xh, rs, cs] = (rate * (total - f32(vb, b, rs, cs))).astype(BF)

    def reduce_job(tag, q, rs, cs, rank, P4, R, first, pieces, names, after, after_cost, after_starts, more=()):
        ring, ahead, behind, far, mine, other = pieces
        up, down, side = names
        u = (rs.stop - rs.start) * (cs.stop - cs.start) / (SH * W) / 8.0

        def part_at(i, half):
            return P4(i, half)

        def slot(k):
            return R.at[q, k, rs, cs]

        n = lambda k: (tag, q, rank, k)
        job = (tag[0], q)
        if job not in sends:
            send_group(job, R.at[q])
        group(n("D1"), R.at[q, pl.ds(0, 2), rs, cs])
        group(n("A"), R.at[q, pl.ds(0, 3), rs, cs])
        group(n("B"), R.at[q, pl.ds(0, 2), rs, cs])
        copy(n("D1p"), up, part_at(far, mine), slot(0), u, job, n("D1"))
        copy(n("D1m"), down, part_at(far, other), slot(1), u, job, n("D1"))
        copy(n("D2pA"), up, part_at(ahead, mine), slot(2), u, job, n("A"))
        copy(n("D2pB"), up, part_at(ahead, other), slot(3), u, job, n("B"))
        copy(n("D2mA"), down, part_at(behind, mine), slot(4), u, job, n("A"))
        copy(n("D2mB"), down, part_at(behind, other), slot(5), u, job, n("B"))
        copy(n("DX"), side, part_at(ring, other), slot(6), u, job, n("A"))

        def add(ref, *slots):
            total = ref[...].astype(F32)
            for k in slots:
                total = total + R[q, k, rs, cs].astype(F32)
            return total

        def s1():
            ref = part_at(ahead, mine)
            ref[...] = add(ref, 0).astype(BF)
            ref = part_at(behind, other)
            ref[...] = add(ref, 1).astype(BF)

        def s2():
            ref = part_at(ring, other)
            ref[...] = add(ref, 3, 5).astype(BF)

        def s3():
            after(rs, cs, add(part_at(ring, mine), 2, 4, 6))

        vpu = u * 8 * 0.1 + 0.03
        task(n("s1"), [first], [n("D1")], 2 * vpu, s1, [n("D2pA"), n("D2mB")], rank)
        task(n("s2"), [n("s1")], [n("B")], vpu, s2, [n("DX")], rank)
        task(n("s3"), [n("s2")], [n("A")], vpu + after_cost, s3, after_starts, rank)
        tasks[-1].needs.extend(more)
        return [n("D1p"), n("D1m"), n("D2pB"), n("D2mA")], n("s3")

    def gather_job(tag, q, rs, cs, rank, F4, R, pieces, names):
        ring, ahead, behind, _, mine, other = pieces
        up, down, side = names
        u = (rs.stop - rs.start) * (cs.stop - cs.start) / (SH * W) / 8.0
        n = lambda k: (tag, q, rank, k)
        job = (tag[0], q)
        group(n("G"), R.at[q, pl.ds(0, 4), rs, cs])
        copy(n("GX"), side, F4(ring, mine), F4(ring, mine), u, job)
        copy(n("Gop"), up, F4(ring, mine), F4(ring, mine), u, job)
        copy(n("Gom"), down, F4(ring, mine), F4(ring, mine), u, job, n("G"))
        copy(n("Gtp"), up, F4(ring, other), F4(ring, other), u, job, n("G"))
        copy(n("Gtm"), down, F4(ring, other), F4(ring, other), u, job)
        copy(n("Fp"), up, F4(behind, mine), F4(behind, mine), u, job, n("G"))
        copy(n("Fm"), down, F4(ahead, other), F4(ahead, other), u, job, n("G"))

        def follow(last):
            task(n("s4"), [last], [n("GX")], 0.05, None, [n("Gtp"), n("Gtm")], rank)
            task(n("s5p"), [last], [n("Gop")], 0.05, None, [n("Fp")], rank)
            task(n("s5m"), [last], [n("Gtm")], 0.05, None, [n("Fm")], rank)
            task(n("end"), [n("s4"), n("s5p"), n("s5m")], [n("G")], 0.05, None, [], rank)
            return n("end")

        return [n("GX"), n("Gop"), n("Gom")], follow

    z_ring, z_names = (z, zp, zm, z2, xh, xo), ("z+", "z-", "xh")
    y_ring, y_names = (y, yp, ym, y2, xl, lo), ("y+", "y-", "xl")

    def col_sends(q):
        if ("c", q) not in sends:
            send_group(("c", q), rbuf.at[pl.ds(0, 2)])

    def col_z(q, rs, cs, rank, first, more):
        def P4(i, half):
            return part.at[q, i, half, rs, cs]

        def F4(i, half):
            return full.at[q, i, half, rs, cs]

        col_sends(q)
        begin, follow = gather_job("cz", q, rs, cs, rank, F4, rbuf, z_ring, z_names)
        starts, last = reduce_job(
            "cz", q, rs, cs, rank, P4, rbuf, first, z_ring, z_names,
            lambda rs, cs, total: finish(q, cs, rs, total), 0.1, begin, more,
        )
        return starts, follow(last)

    def keys_job(rank, first):
        rs, cs = slice(0, SH), slice(0, 128)

        def P4(i, half):
            return gpart.at[i, half]

        def F4(i, half):
            return gfull.at[half, i]

        def store(rs, cs, total):
            gfull[xl, y] = total.astype(BF)

        send_group(("k", 0), rbuf.at[pl.ds(0, 2), :, rs, cs])
        begin, follow = gather_job("kk", 0, rs, cs, rank, F4, gbuf, y_ring, y_names)
        starts, last = reduce_job("kk", 0, rs, cs, rank, P4, gbuf, first, z_ring, z_names, store, 0.0, begin)
        return starts, follow(last)

    def col_x(q, rs, cs, rank, first, more):
        u = (rs.stop - rs.start) * (cs.stop - cs.start) / (SH * W) / 8.0
        half = (cs.stop - cs.start) // 2
        cl, cr = slice(cs.start, cs.start + half), slice(cs.start + half, cs.stop)
        n = lambda k: ("cx", q, rank, k)

        def P3(i, c):
            return part.at[q, i, xh, rs, c]

        def F3(i, c):
            return full.at[q, i, xh, rs, c]

        def slot(k, c):
            return rbuf.at[q, k, rs, c]

        job = ("c", q)
        col_sends(q)
        group(n("D1"), slot(4, cs))
        group(n("D2"), rbuf.at[q, pl.ds(0, 2), rs, cs])
        group(n("F"), slot(4, cs))
        group(n("X"), rbuf.at[q, pl.ds(0, 4), rs, cs])
        copy(n("DX"), "xh", part.at[q, :, xo, rs, cs], rbuf.at[q, pl.ds(0, 4), rs, cs], 4 * u, job)
        copy(n("D1p"), "z+", P3(z2, cl), slot(4, cl), u / 2, job, n("D1"))
        copy(n("D1m"), "z-", P3(z2, cr), slot(4, cr), u / 2, job, n("D1"))
        copy(n("D2pL"), "z+", P3(zp, cl), slot(5, cl), u / 2, job, n("D2"))
        copy(n("D2pR"), "z+", P3(zp, cr), slot(5, cr), u / 2, job, n("D2"))
        copy(n("D2mL"), "z-", P3(zm, cl), slot(6, cl), u / 2, job, n("D2"))
        copy(n("D2mR"), "z-", P3(zm, cr), slot(6, cr), u / 2, job, n("D2"))
        copy(n("Gp"), "z+", F3(z, cs), F3(z, cs), u, job)
        copy(n("Gm"), "z-", F3(z, cs), F3(z, cs), u, job)
        copy(n("Fp"), "z+", F3(zm, cl), F3(zm, cl), u / 2, job, n("F"))
        copy(n("Fm"), "z-", F3(zp, cr), F3(zp, cr), u / 2, job, n("F"))
        copy(n("X0"), "xh", F3(z, cs), F3(z, cs), u, job, n("X"))
        copy(n("Xm"), "xh", F3(zm, cs), F3(zm, cs), u, job, n("X"))
        copy(n("Xp"), "xh", F3(zp, cs), F3(zp, cs), u, job, n("X"))
        copy(n("X2"), "xh", F3(z2, cs), F3(z2, cs), u, job, n("X"))

        def s1():
            for i in range(4):
                part[q, i, xh, rs, cs] = (f32(part, q, i, xh, rs, cs) + f32(rbuf, q, i, rs, cs)).astype(BF)

        def s2():
            part[q, zp, xh, rs, cl] = (f32(part, q, zp, xh, rs, cl) + f32(rbuf, q, 4, rs, cl)).astype(BF)
            part[q, zm, xh, rs, cr] = (f32(part, q, zm, xh, rs, cr) + f32(rbuf, q, 4, rs, cr)).astype(BF)

        def s3():
            finish(q, cs, rs, f32(part, q, z, xh, rs, cs) + f32(rbuf, q, 5, rs, cs) + f32(rbuf, q, 6, rs, cs))

        vpu = u * 8 * 0.1 + 0.03
        task(n("s1"), [first], [n("DX")], 2 * vpu, s1, [n("D1p"), n("D1m"), n("D2pR"), n("D2mL")], rank)
        task(n("s2"), [n("s1")], [n("D1")], 2 * vpu, s2, [n("D2pL"), n("D2mR")], rank)
        task(n("s3"), [n("s2"), *more], [n("D2")], vpu + 0.1, s3, [n("Gp"), n("Gm"), n("X0")], rank)
        task(n("s4p"), [n("s3")], [n("Gp")], 0.05, None, [n("Fp"), n("Xm")], rank)
        task(n("s4m"), [n("s3")], [n("Gm")], 0.05, None, [n("Fm"), n("Xp")], rank)
        task(n("s5"), [n("s4p"), n("s4m")], [n("F")], 0.05, None, [n("X2")], rank)
        task(n("end"), [n("s5")], [n("X")], 0.05, None, [], rank)
        return [n("DX")], n("end")

    def row_job(u, rs, cs, rank, first):
        def P4(i, half):
            return part2.at[u, half, i, rs, cs]

        def store(rs, cs, total):
            i, b = u // 2, u % 2
            ref, hbm = ((qg_ref, qg_hbm), (kg_ref, kg_hbm))[i]
            ref[0, b, rs, cs] = total.astype(BF)
            out(i, ref, hbm, 0, b, rs, cs)

        return reduce_job(
            "r", u, rs, cs, rank, P4, rbuf2, first, y_ring, y_names, store, 0.0, [],
        )

    def dot(a, b, dims=None):
        if dims is None:
            return jnp.dot(a, b, preferred_element_type=F32)
        return lax.dot_general(a, b, dims, preferred_element_type=F32)

    def whole(ref, *index):
        return ref[index].reshape(8 * SH, -1)

    def some(ref, *index):
        return ref[index].reshape(8 * RW, W)

    ends = [[None] * NJ for _ in range(4)]
    everything = slice(0, SH)
    full_cols = slice(0, W)

    def cols(g):
        return slice(g * CW, (g + 1) * CW)

    def toks(k):
        return slice(k * RW, (k + 1) * RW)

    def spread(q, block, width, value, rs, cs):
        part[q, :, :, rs, cs] = value.astype(BF).reshape(4, 2, rs.stop - rs.start, cs.stop - cs.start)

    def phase_a(q, g, rank):
        b, src, half = (1, cf, ch) if q == 0 else (0, mf, mh0)
        rs, cs = everything, cols(g)
        name = ("P", q, g)

        def body():
            need("K1" if q == 0 else "K0", ("C" if q == 0 else "M", g))
            half[cs, :] = src[cs, :].astype(BF)
            spread(q, g, CW, dot(whole(kb, b), half[cs, :], NT), rs, cs)

        make = col_x if (q, g) in X_FIRST else col_z
        starts, ends[q][g] = make(q, rs, cs, rank, name, [])
        task(name, [], [], 0.35, body, starts, rank)

    for i, (q, g) in enumerate([(0, g) for g in range(NJ)] + [(1, g) for g in range(NJ)]):
        phase_a(q, g, i)

    def keys_product():
        name = ("KK",)

        def body():
            need("K0", "K1")
            odd = y % 2
            rhs = kb[odd, pl.ds(2 * (row // 2), 2)].reshape(128, W)
            value = dot(kb[1 - odd].reshape(8 * SH, W), rhs, NT)
            gpart[...] = value.astype(BF).reshape(4, 2, SH, 128)

        starts, end = keys_job(7.2, name)
        task(name, [], [], 0.4, body, starts, 7.2)
        return end

    keys_end = keys_product()

    def correction(q, g):
        cs = cols(g)
        src, odd = (0, 1) if q == 2 else (1, 0)

        def body():
            lhs = jnp.concatenate([gfull[r // 4, r % 4] for r in range(odd, 8, 2)], axis=1)
            fix[q - 2, :, cs] = dot(lhs, full[src, :, :, :, cs].reshape(8 * SH, CW))

        task(("FX", q, g), [keys_end, ends[src][g]], [], 0.08, body, [], 7.4 if q == 2 else 8.4)

    def project_known(g):
        cs = cols(g)

        def body():
            need("Y1", "Q1")
            step = dot(yb[1, :, :, cs].reshape(8 * SH, CW), whole(qb, 1), TN)
            before = cf[cs, :]
            cf[cs, :] = 0.999 * before + step
            ph0[cs, :] = (1.899 * before + step).astype(BF)

        task(("PK", g), [("P", 0, g)], [], 0.35, body, [], 7.1)

    def project_update(g):
        cs = cols(g)

        def body():
            step = dot(full[0, :, :, :, cs].reshape(8 * SH, CW), whole(kb, 1), TN)
            adjoint = cf[cs, :] + step
            cf[cs, :] = adjoint
            ph0[cs, :] = (adjoint + 0.9 * ch[cs, :].astype(F32)).astype(BF)

        task(("PU", g), [ends[0][g]] + [("P", 2, k) for k in range(NJ)], [], 0.45, body, [], 16.1)

    def memory_update(g):
        cs = cols(g)

        def body():
            need("K0")
            step = dot(full[1, :, :, :, cs].reshape(8 * SH, CW), whole(kb, 0), TN)
            mh1[cs, :] = (0.999 * mf[cs, :] - step).astype(BF)

        task(("MU", g), [ends[1][g]], [], 0.38, body, [], 16.2)

    for g in range(NJ):
        project_known(g)
        correction(2, g)
        correction(3, g)
        project_update(g)
        memory_update(g)
    all_pu = [("PU", g) for g in range(NJ)]
    all_mu = [("MU", g) for g in range(NJ)]

    def query_part(u, g, rank):
        mem = mh0 if u == 0 else mh1
        rs, cs = everything, slice(g * W // NQ, (g + 1) * W // NQ)
        name = ("QP", u, g)

        def body():
            need("Y%d" % u)
            for lo in range(cs.start, cs.stop, CW):
                value = dot(whole(yb, u), mem[:, lo : lo + CW])
                part2[u, :, :, rs, lo : lo + CW] = value.astype(BF).reshape(2, 4, SH, CW)

        starts, _ = row_job(u, rs, cs, rank, name)
        deps = [("P", 1, g) for g in range(NJ)] if u == 0 else all_mu
        task(name, deps, [], 0.6, body, starts, rank)

    for g in range(NQ):
        query_part(0, g, 20 + g)
        query_part(1, g, 24 + g)

    def phase_b(q, k, rank):
        b, half = (0, ph0) if q == 2 else (1, mh0)
        deps = [("PK", g) if q == 2 else ("P", 1, g) for g in range(NJ)]
        rs, cs = toks(k), full_cols
        name = ("P", q, k)

        def body():
            need("K%d" % b)
            lhs = some(kb, b, slice(None), rs)
            for n in range(NJ):
                spread(q, n, CW, dot(lhs, half[cols(n), :], NT), rs, cols(n))

        make = col_x if (q, k) in X_FIRST else col_z
        starts, ends[q][k] = make(q, rs, cs, rank, name, [("FX", q, g) for g in range(NJ)])
        task(name, deps, [], 0.7, body, starts, rank)

    for i, (q, k) in enumerate([(2, k) for k in range(NJ)] + [(3, k) for k in range(NJ)]):
        phase_b(q, k, 8 + i)

    def key_part(u, k, rank):
        rs = toks(k)
        f, w, mem, proj = (2, 1, mh0, ph0) if u == 2 else (0, 3, mh1, ch)
        name = ("KP", u, k)

        def body():
            err, wgt = some(full, f, slice(None), slice(None), rs), some(full, w, slice(None), slice(None), rs)
            for n in range(NJ):
                value = dot(err, mem[:, cols(n)]) - dot(wgt, proj[:, cols(n)])
                part2[u, :, :, rs, cols(n)] = value.astype(BF).reshape(2, 4, RW, CW)

        starts, _ = row_job(u, rs, full_cols, rank, name)
        deps = [ends[2][k]] + all_pu + all_mu if u == 2 else [ends[3][k]] + all_pu + all_mu
        task(name, deps, [], 0.65, body, starts, rank)

    for k in range(NJ):
        key_part(2, k, 17 + k / 10)
        key_part(3, k, 18 + k / 10)

    def adjoint_early(g):
        cs = cols(g)

        def body():
            need("Y0", "Q0")
            cf[cs, :] = 0.999 * cf[cs, :] + dot(yb[0, :, :, cs].reshape(8 * SH, CW), whole(qb, 0), TN)

        task(("AE", g), [("PU", g)], [], 0.38, body, [], 30)

    def adjoint_late(g):
        cs = cols(g)

        def body():
            step = dot(full[2, :, :, :, cs].reshape(8 * SH, CW), whole(kb, 0), TN)
            qb[g // 2, four] = (cf[cs, :] + step).astype(BF).reshape(4, SH, W)

        four = slice(g % 2 * 4, g % 2 * 4 + 4)
        copy(("A", g), "dp", qb.at[g // 2, four], arec.at[g // 2, four], 0.5, "A")
        task(("AL", g), [("AE", h) for h in range(NJ)] + ends[2], [], 0.38, body, [("A", g)], 19)

        def total():
            cf[cs, :] = (qb[g // 2, four].astype(F32) + arec[g // 2, four].astype(F32)).reshape(CW, W)
            out(3, cf, ig_hbm, cs)

        task(("AT", g), [("AL", g)], [("A", g)], 0.1, total, [], 31)

    for g in range(NJ):
        adjoint_early(g)
    send_group("A", arec)
    for g in range(NJ):
        adjoint_late(g)

    order, _ = order_tasks(tasks, links, sizes)
    if ORDER:
        order = [tasks[i] for i in ORDER]
    held = []
    for item in order:
        if held is not None and (item.groups or len(held) == 6):
            pl.semaphore_wait(barrier, len(device))
            for name in [name for early in held for name in early.starts]:
                copies[name].start()
            held = None
        for name in item.groups:
            groups[name][0].wait()
        if item.body is not None:
            item.body()
        if held is not None:
            held.append(item)
            continue
        for name in item.starts:
            copies[name].start()
    for wait, _ in sends.values():
        wait.wait()
    for i, (ref, hbm) in enumerate(((qg_ref, qg_hbm), (kg_ref, kg_hbm), (vg_ref, vg_hbm), (cf, ig_hbm))):
        pltpu.make_async_copy(ref, hbm, osem.at[i]).wait()


def on_device(query, key, value, out_grad, rate, memory_init, memory_cot):
    shared = (1, 2, 8, SH, W)
    vm = pltpu.VMEM
    n_recv, n_send = 17 * 7 + (2 * NQ + 8) * 3 + NJ, 10
    outs = pl.pallas_call(
        kernel,
        out_shape=(
            jax.ShapeDtypeStruct((1, 2, SH, W), BF),
            jax.ShapeDtypeStruct((1, 2, SH, W), BF),
            jax.ShapeDtypeStruct((1, 2, SH, W), BF),
            jax.ShapeDtypeStruct((W, W), F32),
        ),
        in_specs=[pl.BlockSpec(memory_space=pltpu.HBM)] * 7,
        out_specs=(pl.BlockSpec(memory_space=pl.ANY),) * 4,
        scratch_shapes=[
            vm((1, 2, SH, W), BF),
            vm((1, 2, SH, W), BF),
            vm((1, 2, SH, W), BF),
            vm((W, W), F32),
            vm((2, 8, SH, W), BF),
            vm((2, 8, SH, W), BF),
            vm((2, 8, SH, W), BF),
            vm((2, SH, W), BF),
            vm((1, 2, 8 * SH), F32),
            vm((W, W), F32),
            vm((W, W), BF),
            vm((W, W), BF),
            vm((W, W), BF),
            vm((W, W), BF),
            vm((4, 4, 2, SH, W), BF),
            vm((4, 4, 2, SH, W), BF),
            vm((4, 7, SH, W), BF),
            vm((4, 2, 4, SH, W), BF),
            vm((4, 7, SH, W), BF),
            vm((2, 8, SH, W), BF),
            vm((2, SH, 128), F32),
            vm((4, 2, SH, 128), BF),
            vm((2, 4, SH, 128), BF),
            vm((1, 7, SH, 128), BF),
            vm((2, SH, W), F32),
            pltpu.SemaphoreType.DMA((n_send,)),
            pltpu.SemaphoreType.DMA((n_recv,)),
            pltpu.SemaphoreType.DMA((16,)),
            pltpu.SemaphoreType.DMA((4,)),
        ],
        compiler_params=pltpu.CompilerParams(
            collective_id=0, has_side_effects=True, vmem_limit_bytes=56 * 2**20
        ),
        name="memory_backward",
    )(
        query.reshape(shared), key.reshape(shared), value.reshape(shared), out_grad.reshape(shared), rate,
        memory_init, memory_cot,
    )
    return publish(*outs)


def publish_kernel(*refs):
    ins, outs, held, (rsem, wsem) = refs[:4], refs[4:8], refs[8:12], refs[12:]
    whole = [(ins[i], held[i], outs[i]) for i in range(3)]
    rows = [pl.ds(g * 128, 128) for g in range(8)]
    parts = [(ins[3].at[r], held[3].at[r], outs[3].at[r]) for r in rows] + whole
    reads = [pltpu.make_async_copy(a, b, rsem.at[i]) for i, (a, b, _) in enumerate(parts)]
    writes = [pltpu.make_async_copy(b, c, wsem.at[i]) for i, (_, b, c) in enumerate(parts)]
    for read in reads:
        read.start()
    for read, write in zip(reads, writes):
        read.wait()
        write.start()
    for write in writes:
        write.wait()


def publish(*arrays):
    shapes = tuple(jax.ShapeDtypeStruct(a.shape, a.dtype) for a in arrays)
    return pl.pallas_call(
        publish_kernel,
        out_shape=shapes,
        in_specs=[pl.BlockSpec(memory_space=pl.ANY)] * 4,
        out_specs=(pl.BlockSpec(memory_space=pl.ANY),) * 4,
        scratch_shapes=[pltpu.VMEM(a.shape, a.dtype) for a in arrays]
        + [pltpu.SemaphoreType.DMA((11,)), pltpu.SemaphoreType.DMA((11,))],
        compiler_params=pltpu.CompilerParams(vmem_limit_bytes=60 * 2**20),
        name="publish",
    )(*arrays)


def solution(mesh):
    placed = (
        P("dp", None, None, "col"),
        P("dp", None, None, "col"),
        P("dp", None, None, "row"),
        P("dp", None, None, "row"),
        P("dp", None, None),
        P("row", "col"),
        P("row", "col"),
    )
    return jax.shard_map(
        on_device,
        mesh=mesh,
        in_specs=placed,
        out_specs=(
            P("dp", None, "row", "col"),
            P("dp", None, "row", "col"),
            P("dp", None, "col", "row"),
            P("row", "col"),
        ),
        check_vma=False,
    )
```

```python
import functools

import jax
import jax.numpy as jnp
from jax import lax
from jax.experimental import pallas as pl
from jax.experimental.pallas import tpu as pltpu
from jax.sharding import PartitionSpec as P

MESH = pl.DeviceIdType.MESH
BF, F32 = jnp.bfloat16, jnp.float32
W = 1024
SH = 64
NJ = 4
NQ = 2
CW, RW = W // NJ, SH // NJ
ALL = slice(0, W)
X_FIRST = frozenset([(0, 0), (0, 3), (1, 0), (1, 1), (1, 2), (2, 3)])
ROW_X_FIRST = frozenset([(2, 3), (3, 3)])
UNIT_US = 23.4
HOP_US = {"z+": 2.7, "z-": 2.7, "y+": 2.7, "y-": 2.7, "x": 3.7, "dp": 1.1}
CORE = 1.0
NT = (((1,), (1,)), ((), ()))
TN = (((0,), (0,)), ((), ()))
ORDER = (
    15, 7, 68, 23, 31, 63, 39, 47, 55, 104, 174, 69, 166, 64, 79, 0, 8, 16, 84, 56, 24, 74, 134, 1,
    9, 32, 118, 17, 142, 25, 40, 126, 96, 57, 33, 2, 48, 127, 26, 92, 18, 65, 41, 10, 34, 49, 3, 111,
    4, 28, 135, 100, 27, 19, 42, 11, 58, 36, 50, 35, 12, 66, 119, 128, 20, 21, 29, 5, 112, 44, 13, 43,
    159, 158, 37, 120, 136, 51, 52, 150, 22, 67, 167, 80, 45, 6, 30, 85, 82, 14, 75, 59, 70, 129, 87, 60,
    151, 97, 113, 53, 160, 38, 143, 168, 71, 61, 73, 137, 72, 101, 152, 130, 46, 121, 114, 210, 76, 144, 93, 131,
    54, 81, 62, 86, 161, 169, 139, 108, 132, 89, 83, 138, 115, 78, 153, 122, 116, 145, 98, 77, 102, 123, 133, 162,
    163, 88, 170, 194, 105, 171, 124, 140, 154, 117, 178, 155, 94, 146, 207, 164, 172, 147, 191, 90, 125, 186, 106, 156,
    141, 202, 175, 148, 165, 198, 208, 103, 95, 173, 206, 183, 157, 190, 149, 182, 107, 209, 211, 213, 195, 215, 187, 176,
    212, 109, 179, 184, 99, 192, 199, 203, 196, 188, 180, 200, 217, 204, 177, 216, 185, 189, 214, 218, 110, 91, 197, 201,
    193, 205, 181,
)


class Task:
    def __init__(self, name, needs, groups, waits, cost, body, starts, rank):
        self.name, self.needs, self.groups, self.waits, self.cost = name, needs, groups, waits, cost
        self.body, self.starts, self.rank = body, starts, rank


def order_tasks(tasks, links, sizes):
    free, arrive, done, now = {}, {}, {}, 0.0
    left, result = list(tasks), []
    while left:
        best = None
        for task in left:
            if any(n not in done for n in task.needs) or any(w not in arrive for w in task.waits):
                continue
            ready = max([now] + [done[n] for n in task.needs] + [arrive[w] for w in task.waits])
            key = (ready, task.rank)
            if best is None or key < best[0]:
                best = (key, task)
        (ready, _), task = best
        now = ready + CORE * task.cost + 0.03 * len(task.starts)
        done[task.name] = now
        for copy in task.starts:
            link = links[copy]
            begin = max(now, free.get(link, 0.0))
            free[link] = begin + sizes[copy]
            arrive[copy] = free[link] + HOP_US[link]
        left.remove(task)
        result.append(task)
    return result, now


def kernel(
    q_hbm, k_hbm, v_hbm, y_hbm, r_hbm, m_hbm, c_hbm,
    qg_hbm, kg_hbm, vg_hbm, ig_hbm,
    qg_ref, kg_ref, vg_ref, cf, kb, qb, yb, vb, rb, mf, mh0, mh1, ch, ph0, part, full, rbuf, part2, rbuf2, arec, rc, gpart, gfull, gbuf, fix, upart, ufull, ubuf, q1,
    ssem, rsem, lsem, osem,
):
    dp, row, col = lax.axis_index("dp"), lax.axis_index("row"), lax.axis_index("col")
    z, xh = col // 2, col % 2
    xl, y = row // 4, row % 4
    zp, zm, z2, xo = (z + 1) % 4, (z + 3) % 4, (z + 2) % 4, 1 - xh
    yp, ym, y2, lo = (y + 1) % 4, (y + 3) % 4, (y + 2) % 4, 1 - xl
    device = {
        "z+": (dp, row, zp * 2 + xh),
        "z-": (dp, row, zm * 2 + xh),
        "xh": (dp, row, z * 2 + xo),
        "y+": (dp, xl * 4 + yp, col),
        "y-": (dp, xl * 4 + ym, col),
        "xl": (dp, lo * 4 + y, col),
        "y2": (dp, xl * 4 + y2, col),
        "z2": (dp, row, z2 * 2 + xh),
        "dp": (1 - dp, row, col),
    }

    loads = {}

    def load(name, src, dst):
        loads[name] = pltpu.make_async_copy(src, dst, lsem.at[len(loads)])

    def rows_of(g):
        return pl.ds(g * CW, CW)

    load("K1", k_hbm.at[0, 1], kb.at[1])
    for g in range(NJ):
        load(("C", g), c_hbm.at[rows_of(g)], cf.at[rows_of(g)])
    load("K0", k_hbm.at[0, 0], kb.at[0])
    for g in range(NJ):
        load(("M", g), m_hbm.at[rows_of(g)], mf.at[rows_of(g)])
    load("Y1", y_hbm.at[0, 1], yb.at[1])
    load("Q1", q_hbm.at[0, 1], qb.at[1])
    load("R", r_hbm, rb)
    load("V", v_hbm.at[0, :, col], vb)
    load("Y0", y_hbm.at[0, 0], yb.at[0])
    load("Q0", q_hbm.at[0, 0], qb.at[0])
    loaded = set()
    stages = [
        ["K1"] + [("C", g) for g in range(NJ)],
        ["K0"] + [("M", g) for g in range(NJ)],
        ["Y1", "Q1", "R", "V", "Y0", "Q0"],
    ]

    def next_stage():
        for name in stages.pop(0):
            loads[name].start()

    def need(*names):
        for name in names:
            if name in loaded:
                continue
            while any(name in stage for stage in stages):
                next_stage()
            loads[name].wait()
            loaded.add(name)
            if stages and name in (("C", 0), ("M", 0)):
                next_stage()

    next_stage()

    barrier = pltpu.get_barrier_semaphore()
    for partner in device.values():
        pl.semaphore_signal(barrier, inc=1, device_id=partner, device_id_type=MESH)

    def rates():
        need("R")
        at = lax.broadcasted_iota(jnp.int32, (SH, 8 * SH), 1)
        own = lax.broadcasted_iota(jnp.int32, (SH, 8 * SH), 0) + col * SH
        for b in range(2):
            picked = jnp.where(at == own, jnp.broadcast_to(rb[0, b : b + 1, :], (SH, 8 * SH)), 0.0)
            rc[b] = jnp.broadcast_to(jnp.sum(picked, axis=1, keepdims=True), (SH, 128))

    copies, links, sizes, groups, sends = {}, {}, {}, {}, {}

    def waiter(ref, sem):
        return pltpu.make_async_copy(ref, ref, sem)

    def send_group(key, ref):
        sends[key] = waiter(ref, ssem.at[len(sends)]), ssem.at[len(sends)]

    def group(name, ref):
        groups[name] = waiter(ref, rsem.at[len(groups)]), rsem.at[len(groups)]

    def copy(name, link, src, dst, units, job, into=None, over=None):
        if into is None:
            group(name, dst)
            into = name
        copies[name] = pltpu.make_async_remote_copy(
            src_ref=src, dst_ref=dst, send_sem=sends[job][1], recv_sem=groups[into][1],
            device_id=device[link], device_id_type=MESH,
        )
        members.setdefault(into, []).append(name)
        links[name] = over or ("x" if link in ("xh", "xl") else link)
        sizes[name] = units * (UNIT_US if link != "dp" else 1.2)

    members = {}

    tasks = []

    def task(name, needs, waits, cost, body, starts, rank):
        tasks.append(Task(name, needs, waits, [c for w in waits for c in members[w]], cost, body, starts, rank))

    def out(i, ref, hbm, *index):
        pltpu.make_async_copy(ref.at[index], hbm.at[index], osem.at[i]).start()

    def f32(ref, *index):
        return ref[index].astype(F32)

    def finish(q, cs, rs, total):
        if "V" not in loaded:
            rates()
        need("V")
        b = 1 if q in (0, 3) else 0
        rate = jnp.broadcast_to(rc[b, rs, 0:1], total.shape)
        if q == 2:
            total = total + fix[0, rs, cs]
        if q == 3:
            total = 0.999 * total - fix[1, rs, cs]
        if q in (0, 2):
            scaled = (rate * total).astype(BF)
            vg_ref[0, b, rs, cs] = scaled
            out(2, vg_ref, vg_hbm, 0, b, rs, cs)
            full[q, z, xh, rs, cs] = -scaled
        else:
            full[q, z, xh, rs, cs] = (rate * (total - f32(vb, b, rs, cs))).astype(BF)

    def reduce_job(tag, q, rs, cs, rank, P4, R, first, pieces, names, after, after_cost, after_starts, more=()):
        ring, ahead, behind, far, mine, other = pieces
        up, down, side = names
        u = (rs.stop - rs.start) * (cs.stop - cs.start) / (SH * W) / 8.0

        def part_at(i, half):
            return P4(i, half)

        def slot(k):
            return R.at[q, k, rs, cs]

        n = lambda k: (tag, q, rank, k)
        job = (tag[0], q)
        if job not in sends:
            send_group(job, R.at[q])
        group(n("D1"), R.at[q, pl.ds(0, 2), rs, cs])
        group(n("A"), R.at[q, pl.ds(0, 3), rs, cs])
        group(n("B"), R.at[q, pl.ds(0, 2), rs, cs])
        copy(n("D1p"), up, part_at(far, mine), slot(0), u, job, n("D1"))
        copy(n("D1m"), down, part_at(far, other), slot(1), u, job, n("D1"))
        copy(n("D2pA"), up, part_at(ahead, mine), slot(2), u, job, n("A"))
        copy(n("D2pB"), up, part_at(ahead, other), slot(3), u, job, n("B"))
        copy(n("D2mA"), down, part_at(behind, mine), slot(4), u, job, n("A"))
        copy(n("D2mB"), down, part_at(behind, other), slot(5), u, job, n("B"))
        copy(n("DX"), side, part_at(ring, other), slot(6), u, job, n("A"))

        def add(ref, *slots):
            total = ref[...].astype(F32)
            for k in slots:
                total = total + R[q, k, rs, cs].astype(F32)
            return total

        def s1():
            ref = part_at(ahead, mine)
            ref[...] = add(ref, 0).astype(BF)
            ref = part_at(behind, other)
            ref[...] = add(ref, 1).astype(BF)

        def s2():
            ref = part_at(ring, other)
            ref[...] = add(ref, 3, 5).astype(BF)

        def s3():
            after(rs, cs, add(part_at(ring, mine), 2, 4, 6))

        vpu = u * 8 * 0.1 + 0.03
        task(n("s1"), [first], [n("D1")], 2 * vpu, s1, [n("D2pA"), n("D2mB")], rank)
        task(n("s2"), [n("s1")], [n("B")], vpu, s2, [n("DX")], rank)
        task(n("s3"), [n("s2")], [n("A")], vpu + after_cost, s3, after_starts, rank)
        tasks[-1].needs.extend(more)
        return [n("D1p"), n("D1m"), n("D2pB"), n("D2mA")], n("s3")

    def gather_job(tag, q, rs, cs, rank, F4, R, pieces, names):
        ring, ahead, behind, _, mine, other = pieces
        up, down, side = names
        u = (rs.stop - rs.start) * (cs.stop - cs.start) / (SH * W) / 8.0
        n = lambda k: (tag, q, rank, k)
        job = (tag[0], q)
        group(n("G"), R.at[q, pl.ds(0, 4), rs, cs])
        copy(n("GX"), side, F4(ring, mine), F4(ring, mine), u, job)
        copy(n("Gop"), up, F4(ring, mine), F4(ring, mine), u, job)
        copy(n("Gom"), down, F4(ring, mine), F4(ring, mine), u, job, n("G"))
        copy(n("Gtp"), up, F4(ring, other), F4(ring, other), u, job, n("G"))
        copy(n("Gtm"), down, F4(ring, other), F4(ring, other), u, job)
        copy(n("Fp"), up, F4(behind, mine), F4(behind, mine), u, job, n("G"))
        copy(n("Fm"), down, F4(ahead, other), F4(ahead, other), u, job, n("G"))

        def follow(last):
            task(n("s4"), [last], [n("GX")], 0.05, None, [n("Gtp"), n("Gtm")], rank)
            task(n("s5p"), [last], [n("Gop")], 0.05, None, [n("Fp")], rank)
            task(n("s5m"), [last], [n("Gtm")], 0.05, None, [n("Fm")], rank)
            task(n("end"), [n("s4"), n("s5p"), n("s5m")], [n("G")], 0.05, None, [], rank)
            return n("end")

        return [n("GX"), n("Gop"), n("Gom")], follow

    z_ring, z_names = (z, zp, zm, z2, xh, xo), ("z+", "z-", "xh")
    y_ring, y_names = (y, yp, ym, y2, xl, lo), ("y+", "y-", "xl")

    def col_sends(q):
        if ("c", q) not in sends:
            send_group(("c", q), rbuf.at[pl.ds(0, 2)])

    def col_z(q, rs, cs, rank, first, more):
        def P4(i, half):
            return part.at[q, i, half, rs, cs]

        def F4(i, half):
            return full.at[q, i, half, rs, cs]

        col_sends(q)
        begin, follow = gather_job("cz", q, rs, cs, rank, F4, rbuf, z_ring, z_names)
        starts, last = reduce_job(
            "cz", q, rs, cs, rank, P4, rbuf, first, z_ring, z_names,
            lambda rs, cs, total: finish(q, cs, rs, total), 0.1, begin, more,
        )
        return starts, follow(last)

    def keys_job(rank, first):
        rs, cs = slice(0, SH), slice(0, 128)

        n = lambda k: ("kk", 0, rank, k)
        u, job = 1 / 64, ("k", 0)
        send_group(job, rbuf.at[pl.ds(0, 2), :, rs, cs])
        group(n("Z"), gbuf.at[0, pl.ds(0, 6)])
        group(n("Y"), gbuf.at[0, pl.ds(0, 6)])
        for i, (there, at, cost) in enumerate((("z+", zp, 1), ("z-", zm, 1), ("z2", z2, 2))):
            over = "z+" if i == 2 else there
            copy(n(there), there, gpart.at[at], gbuf.at[0, pl.ds(2 * i, 2)], 2 * cost * u, job, n("Z"), over)
        copy(n("DX"), "xh", gpart.at[z, xo], gbuf.at[0, 6], u, job)
        copy(n("GX"), "xl", gfull.at[xl, y], gfull.at[xl, y], u, job)
        for there, cost in (("y+", 1), ("y-", 1), ("y2", 2)):
            over = "y+" if there == "y2" else there
            copy(n(there), there, gfull.at[:, y], gfull.at[:, y], 2 * cost * u, job, n("Y"), over)

        def s1():
            for half in (xo, xh):
                total = gpart[z, half].astype(F32)
                for i in range(3):
                    total = total + gbuf[0, 2 * i + half].astype(F32)
                gpart[z, half] = total.astype(BF)

        def s2():
            gfull[xl, y] = (gpart[z, xh].astype(F32) + gbuf[0, 6].astype(F32)).astype(BF)

        task(n("s1"), [first], [n("Z")], 0.1, s1, [n("DX")], rank)
        task(n("s2"), [n("s1")], [n("DX")], 0.06, s2, [n("GX")], rank)
        task(n("s3"), [n("s2")], [n("GX")], 0.06, None, [n("y+"), n("y-"), n("y2")], rank)
        task(n("end"), [n("s3")], [n("Y")], 0.06, None, [], rank)
        return [n("z+"), n("z-"), n("z2")], n("end")

    def col_x(q, rs, cs, rank, first, more):
        u = (rs.stop - rs.start) * (cs.stop - cs.start) / (SH * W) / 8.0
        half = (cs.stop - cs.start) // 2
        cl, cr = slice(cs.start, cs.start + half), slice(cs.start + half, cs.stop)
        n = lambda k: ("cx", q, rank, k)

        def P3(i, c):
            return part.at[q, i, xh, rs, c]

        def F3(i, c):
            return full.at[q, i, xh, rs, c]

        def slot(k, c):
            return rbuf.at[q, k, rs, c]

        job = ("c", q)
        col_sends(q)
        group(n("D1"), slot(4, cs))
        group(n("D2"), rbuf.at[q, pl.ds(0, 2), rs, cs])
        group(n("F"), slot(4, cs))
        group(n("X"), rbuf.at[q, pl.ds(0, 4), rs, cs])
        copy(n("DX"), "xh", part.at[q, :, xo, rs, cs], rbuf.at[q, pl.ds(0, 4), rs, cs], 4 * u, job)
        copy(n("D1p"), "z+", P3(z2, cl), slot(4, cl), u / 2, job, n("D1"))
        copy(n("D1m"), "z-", P3(z2, cr), slot(4, cr), u / 2, job, n("D1"))
        copy(n("D2pL"), "z+", P3(zp, cl), slot(5, cl), u / 2, job, n("D2"))
        copy(n("D2pR"), "z+", P3(zp, cr), slot(5, cr), u / 2, job, n("D2"))
        copy(n("D2mL"), "z-", P3(zm, cl), slot(6, cl), u / 2, job, n("D2"))
        copy(n("D2mR"), "z-", P3(zm, cr), slot(6, cr), u / 2, job, n("D2"))
        copy(n("Gp"), "z+", F3(z, cs), F3(z, cs), u, job)
        copy(n("Gm"), "z-", F3(z, cs), F3(z, cs), u, job)
        copy(n("Fp"), "z+", F3(zm, cl), F3(zm, cl), u / 2, job, n("F"))
        copy(n("Fm"), "z-", F3(zp, cr), F3(zp, cr), u / 2, job, n("F"))
        copy(n("X0"), "xh", F3(z, cs), F3(z, cs), u, job, n("X"))
        copy(n("Xm"), "xh", F3(zm, cs), F3(zm, cs), u, job, n("X"))
        copy(n("Xp"), "xh", F3(zp, cs), F3(zp, cs), u, job, n("X"))
        copy(n("X2"), "xh", F3(z2, cs), F3(z2, cs), u, job, n("X"))

        def s1():
            for i in range(4):
                part[q, i, xh, rs, cs] = (f32(part, q, i, xh, rs, cs) + f32(rbuf, q, i, rs, cs)).astype(BF)

        def s2():
            part[q, zp, xh, rs, cl] = (f32(part, q, zp, xh, rs, cl) + f32(rbuf, q, 4, rs, cl)).astype(BF)
            part[q, zm, xh, rs, cr] = (f32(part, q, zm, xh, rs, cr) + f32(rbuf, q, 4, rs, cr)).astype(BF)

        def s3():
            finish(q, cs, rs, f32(part, q, z, xh, rs, cs) + f32(rbuf, q, 5, rs, cs) + f32(rbuf, q, 6, rs, cs))

        vpu = u * 8 * 0.1 + 0.03
        task(n("s1"), [first], [n("DX")], 2 * vpu, s1, [n("D1p"), n("D1m"), n("D2pR"), n("D2mL")], rank)
        task(n("s2"), [n("s1")], [n("D1")], 2 * vpu, s2, [n("D2pL"), n("D2mR")], rank)
        task(n("s3"), [n("s2"), *more], [n("D2")], vpu + 0.1, s3, [n("Gp"), n("Gm"), n("X0")], rank)
        task(n("s4p"), [n("s3")], [n("Gp")], 0.05, None, [n("Fp"), n("Xm")], rank)
        task(n("s4m"), [n("s3")], [n("Gm")], 0.05, None, [n("Fm"), n("Xp")], rank)
        task(n("s5"), [n("s4p"), n("s4m")], [n("F")], 0.05, None, [n("X2")], rank)
        task(n("end"), [n("s5")], [n("X")], 0.05, None, [], rank)
        return [n("DX")], n("end")

    def row_job(u, rs, cs, rank, first):
        def P4(i, half):
            return part2.at[u, half, i, rs, cs]

        def store(rs, cs, total):
            if u == 1:
                q1[rs, cs] = total
                return
            i, b = u // 2, u % 2
            ref, hbm = ((qg_ref, qg_hbm), (kg_ref, kg_hbm))[i]
            ref[0, b, rs, cs] = total.astype(BF)
            out(i, ref, hbm, 0, b, rs, cs)

        return reduce_job(
            "r", u, rs, cs, rank, P4, rbuf2, first, y_ring, y_names, store, 0.0, [],
        )

    def row_x(u, rs, cs, rank, first):
        share = (rs.stop - rs.start) * (cs.stop - cs.start) / (SH * W) / 8.0
        half = (cs.stop - cs.start) // 2
        cl, cr = slice(cs.start, cs.start + half), slice(cs.start + half, cs.stop)
        n = lambda k: ("rx", u, rank, k)
        job = ("r", u)
        if job not in sends:
            send_group(job, rbuf2.at[u])
        P3 = lambda i, c: part2.at[u, xl, i, rs, c]
        slot = lambda k, c: rbuf2.at[u, k, rs, c]
        group(n("D1"), slot(4, cs))
        group(n("D2"), rbuf2.at[u, pl.ds(0, 2), rs, cs])
        copy(n("DX"), "xl", part2.at[u, lo, :, rs, cs], rbuf2.at[u, pl.ds(0, 4), rs, cs], 4 * share, job)
        copy(n("D1p"), "y+", P3(y2, cl), slot(4, cl), share / 2, job, n("D1"))
        copy(n("D1m"), "y-", P3(y2, cr), slot(4, cr), share / 2, job, n("D1"))
        copy(n("D2pL"), "y+", P3(yp, cl), slot(5, cl), share / 2, job, n("D2"))
        copy(n("D2pR"), "y+", P3(yp, cr), slot(5, cr), share / 2, job, n("D2"))
        copy(n("D2mL"), "y-", P3(ym, cl), slot(6, cl), share / 2, job, n("D2"))
        copy(n("D2mR"), "y-", P3(ym, cr), slot(6, cr), share / 2, job, n("D2"))

        def s1():
            for i in range(4):
                part2[u, xl, i, rs, cs] = (f32(part2, u, xl, i, rs, cs) + f32(rbuf2, u, i, rs, cs)).astype(BF)

        def s2():
            part2[u, xl, yp, rs, cl] = (f32(part2, u, xl, yp, rs, cl) + f32(rbuf2, u, 4, rs, cl)).astype(BF)
            part2[u, xl, ym, rs, cr] = (f32(part2, u, xl, ym, rs, cr) + f32(rbuf2, u, 4, rs, cr)).astype(BF)

        def s3():
            total = f32(part2, u, xl, y, rs, cs) + f32(rbuf2, u, 5, rs, cs) + f32(rbuf2, u, 6, rs, cs)
            kg_ref[0, u - 2, rs, cs] = total.astype(BF)
            out(1, kg_ref, kg_hbm, 0, u - 2, rs, cs)

        task(n("s1"), [first], [n("DX")], 0.1, s1, [n("D1p"), n("D1m"), n("D2pR"), n("D2mL")], rank)
        task(n("s2"), [n("s1")], [n("D1")], 0.06, s2, [n("D2pL"), n("D2mR")], rank)
        task(n("s3"), [n("s2")], [n("D2")], 0.06, s3, [], rank)
        return [n("DX")], n("s3")

    def dot(a, b, dims=None):
        if dims is None:
            return jnp.dot(a, b, preferred_element_type=F32)
        return lax.dot_general(a, b, dims, preferred_element_type=F32)

    def whole(ref, *index):
        return ref[index].reshape(8 * SH, -1)

    def some(ref, *index):
        return ref[index].reshape(8 * RW, W)

    ends = [[None] * NJ for _ in range(4)]
    everything = slice(0, SH)
    full_cols = slice(0, W)

    def cols(g):
        return slice(g * CW, (g + 1) * CW)

    def toks(k):
        return slice(k * RW, (k + 1) * RW)

    def spread(q, block, width, value, rs, cs):
        part[q, :, :, rs, cs] = value.astype(BF).reshape(4, 2, rs.stop - rs.start, cs.stop - cs.start)

    def phase_a(q, g, rank):
        b, src, half = (1, cf, ch) if q == 0 else (0, mf, mh0)
        rs, cs = everything, cols(g)
        name = ("P", q, g)

        def body():
            need("K1" if q == 0 else "K0", ("C" if q == 0 else "M", g))
            half[cs, :] = src[cs, :].astype(BF)
            spread(q, g, CW, dot(whole(kb, b), half[cs, :], NT), rs, cs)

        make = col_x if (q, g) in X_FIRST else col_z
        starts, ends[q][g] = make(q, rs, cs, rank, name, [])
        task(name, [], [], 0.35, body, starts, rank)

    for i, (q, g) in enumerate([(0, g) for g in range(NJ)] + [(1, g) for g in range(NJ)]):
        phase_a(q, g, i)

    def keys_product():
        name = ("KK",)

        def body():
            need("K0", "K1")
            odd = y % 2
            rhs = kb[odd, pl.ds(2 * (row // 2), 2)].reshape(128, W)
            value = dot(kb[1 - odd].reshape(8 * SH, W), rhs, NT)
            gpart[...] = value.astype(BF).reshape(4, 2, SH, 128)

        starts, end = keys_job(7.2, name)
        task(name, [], [], 0.4, body, starts, 7.2)
        return end

    keys_end = keys_product()

    def correction(q, g):
        cs = cols(g)
        src, odd = (0, 1) if q == 2 else (1, 0)

        def body():
            lhs = jnp.concatenate([gfull[r // 4, r % 4] for r in range(odd, 8, 2)], axis=1)
            fix[q - 2, :, cs] = dot(lhs, full[src, :, :, :, cs].reshape(8 * SH, CW))

        task(("FX", q, g), [keys_end, ends[src][g]], [], 0.08, body, [], 7.4 if q == 2 else 8.4)

    def project_known(g):
        cs = cols(g)

        def body():
            need("Y1", "Q1")
            step = dot(yb[1, :, :, cs].reshape(8 * SH, CW), whole(qb, 1), TN)
            before = cf[cs, :]
            cf[cs, :] = 0.999 * before + step
            ph0[cs, :] = (1.899 * before + step).astype(BF)

        task(("PK", g), [("P", 0, g)], [], 0.35, body, [], 7.1)

    def project_update(g):
        cs = cols(g)

        def body():
            step = dot(full[0, :, :, :, cs].reshape(8 * SH, CW), whole(kb, 1), TN)
            adjoint = cf[cs, :] + step
            cf[cs, :] = adjoint
            ph0[cs, :] = (adjoint + 0.9 * ch[cs, :].astype(F32)).astype(BF)

        task(("PU", g), [ends[0][g]] + [("P", 2, k) for k in range(NJ)], [], 0.45, body, [], 16.1)

    def memory_update(g):
        cs = cols(g)

        def body():
            need("K0")
            step = dot(full[1, :, :, :, cs].reshape(8 * SH, CW), whole(kb, 0), TN)
            mh1[cs, :] = (0.999 * mf[cs, :] - step).astype(BF)

        task(("MU", g), [ends[1][g]], [], 0.38, body, [], 16.2)

    for g in range(NJ):
        project_known(g)
        correction(2, g)
        correction(3, g)
        project_update(g)
        memory_update(g)
    all_pu = [("PU", g) for g in range(NJ)]
    all_mu = [("MU", g) for g in range(NJ)]

    def query_part(u, g, rank):
        rs, cs = everything, slice(g * W // NQ, (g + 1) * W // NQ)
        name = ("QP", u, g)

        def body():
            need("Y%d" % u)
            for lo in range(cs.start, cs.stop, CW):
                value = dot(whole(yb, u), mh0[:, lo : lo + CW])
                part2[u, :, :, rs, lo : lo + CW] = value.astype(BF).reshape(2, 4, SH, CW)

        starts, last = row_job(u, rs, cs, rank, name)
        task(name, [("P", 1, g) for g in range(NJ)], [], 0.6, body, starts, rank)

        return last

    for g in range(NQ):
        query_part(0, g, 20 + g)
    q1_sums = [query_part(1, g, 24 + g) for g in range(NQ)]

    def query_update():
        rank, rs, cs = 16.5, slice(0, SH), slice(0, 128)
        n = lambda k: ("u", 0, rank, k)

        def body():
            value = dot(whole(yb, 1), full[1, z].reshape(128, W), NT)
            upart[...] = value.astype(BF).reshape(2, 4, SH, 128)

        def store(rs, cs, total):
            ufull[z] = total.astype(BF)

        send_group(("u", 0), rbuf.at[pl.ds(0, 2), pl.ds(0, 5), rs, cs])
        copy(n("Gp"), "z+", ufull.at[z], ufull.at[z], 1 / 64, ("u", 0))
        group(n("G"), gbuf.at[0, pl.ds(0, 2)])
        copy(n("Gm"), "z-", ufull.at[z], ufull.at[z], 1 / 64, ("u", 0), n("G"))
        copy(n("F"), "z+", ufull.at[zm], ufull.at[zm], 1 / 64, ("u", 0), n("G"))
        starts, last = reduce_job(
            "u", 0, rs, cs, rank, lambda i, half: upart.at[half, i], ubuf, ("UP",), y_ring, y_names, store, 0.0,
            [n("Gp"), n("Gm")],
        )
        task(("UP",), ends[1], [], 0.3, body, starts, rank)
        task(n("s4"), [last], [n("Gp")], 0.05, None, [n("F")], rank)

        def final():
            lhs = jnp.concatenate([ufull[i] for i in range(4)], axis=1)
            for g in range(NJ):
                step = dot(lhs, kb[0, :, :, cols(g)].reshape(8 * SH, CW))
                qg_ref[0, 1, :, cols(g)] = (0.999 * q1[:, cols(g)] - step).astype(BF)
            out(0, qg_ref, qg_hbm, 0, 1)

        task(("QF",), [n("s4")] + q1_sums, [n("G")], 0.3, final, [], 32)

    query_update()

    def phase_b(q, k, rank):
        b, half = (0, ph0) if q == 2 else (1, mh0)
        deps = [("PK", g) if q == 2 else ("P", 1, g) for g in range(NJ)]
        rs, cs = toks(k), full_cols
        name = ("P", q, k)

        def body():
            need("K%d" % b)
            lhs = some(kb, b, slice(None), rs)
            for n in range(NJ):
                spread(q, n, CW, dot(lhs, half[cols(n), :], NT), rs, cols(n))

        make = col_x if (q, k) in X_FIRST else col_z
        starts, ends[q][k] = make(q, rs, cs, rank, name, [("FX", q, g) for g in range(NJ)])
        task(name, deps, [], 0.7, body, starts, rank)

    for i, (q, k) in enumerate([(2, k) for k in range(NJ)] + [(3, k) for k in range(NJ)]):
        phase_b(q, k, 8 + i)

    def key_part(u, k, rank):
        rs = toks(k)
        f, w, mem, proj = (2, 1, mh0, ph0) if u == 2 else (0, 3, mh1, ch)
        name = ("KP", u, k)

        def body():
            err, wgt = some(full, f, slice(None), slice(None), rs), some(full, w, slice(None), slice(None), rs)
            for n in range(NJ):
                value = dot(err, mem[:, cols(n)]) - dot(wgt, proj[:, cols(n)])
                part2[u, :, :, rs, cols(n)] = value.astype(BF).reshape(2, 4, RW, CW)

        starts, _ = (row_x if (u, k) in ROW_X_FIRST else row_job)(u, rs, full_cols, rank, name)
        deps = [ends[2][k]] + all_pu + all_mu if u == 2 else [ends[3][k]] + all_pu + all_mu
        task(name, deps, [], 0.65, body, starts, rank)

    for k in range(NJ):
        key_part(2, k, 17 + k / 10)
        key_part(3, k, 18 + k / 10)

    def adjoint_early(g):
        cs = cols(g)

        def body():
            need("Y0", "Q0")
            cf[cs, :] = 0.999 * cf[cs, :] + dot(yb[0, :, :, cs].reshape(8 * SH, CW), whole(qb, 0), TN)

        task(("AE", g), [("PU", g)], [], 0.38, body, [], 30)

    def adjoint_late(g):
        cs = cols(g)

        def body():
            step = dot(full[2, :, :, :, cs].reshape(8 * SH, CW), whole(kb, 0), TN)
            qb[g // 2, four] = (cf[cs, :] + step).astype(BF).reshape(4, SH, W)

        four = slice(g % 2 * 4, g % 2 * 4 + 4)
        copy(("A", g), "dp", qb.at[g // 2, four], arec.at[g // 2, four], 0.5, "A")
        task(("AL", g), [("AE", h) for h in range(NJ)] + ends[2], [], 0.38, body, [("A", g)], 19)

        def total():
            both = qb[g // 2, four].astype(F32) + arec[g // 2, four].astype(F32)
            ph0[cs, :] = both.astype(BF).reshape(CW, W)
            out(3, ph0, ig_hbm, cs)

        task(("AT", g), [("AL", g)] + [("KP", 2, k) for k in range(NJ)], [("A", g)], 0.1, total, [], 31)

    for g in range(NJ):
        adjoint_early(g)
    send_group("A", arec)
    for g in range(NJ):
        adjoint_late(g)

    order, _ = order_tasks(tasks, links, sizes)
    if ORDER:
        order = [tasks[i] for i in ORDER]
    held = []
    for item in order:
        if held is not None and (item.groups or len(held) == 4):
            pl.semaphore_wait(barrier, len(device))
            for name in [name for early in held for name in early.starts]:
                copies[name].start()
            held = None
        for name in item.groups:
            groups[name][0].wait()
        if item.body is not None:
            item.body()
        if held is not None:
            held.append(item)
            continue
        for name in item.starts:
            copies[name].start()
    for wait, _ in sends.values():
        wait.wait()
    for i, (ref, hbm) in enumerate(((qg_ref, qg_hbm), (kg_ref, kg_hbm), (vg_ref, vg_hbm), (ph0, ig_hbm))):
        pltpu.make_async_copy(ref, hbm, osem.at[i]).wait()


def on_device(query, key, value, out_grad, rate, memory_init, memory_cot):
    shared = (1, 2, 8, SH, W)
    vm = pltpu.VMEM
    n_recv, n_send = 16 * 7 + 4 + (2 * NQ + 8) * 3 + 5 + NJ, 11
    outs = pl.pallas_call(
        kernel,
        out_shape=(
            jax.ShapeDtypeStruct((1, 2, SH, W), BF),
            jax.ShapeDtypeStruct((1, 2, SH, W), BF),
            jax.ShapeDtypeStruct((1, 2, SH, W), BF),
            jax.ShapeDtypeStruct((W, W), BF),
        ),
        in_specs=[pl.BlockSpec(memory_space=pltpu.HBM)] * 7,
        out_specs=(pl.BlockSpec(memory_space=pl.ANY),) * 4,
        scratch_shapes=[
            vm((1, 2, SH, W), BF),
            vm((1, 2, SH, W), BF),
            vm((1, 2, SH, W), BF),
            vm((W, W), F32),
            vm((2, 8, SH, W), BF),
            vm((2, 8, SH, W), BF),
            vm((2, 8, SH, W), BF),
            vm((2, SH, W), BF),
            vm((1, 2, 8 * SH), F32),
            vm((W, W), F32),
            vm((W, W), BF),
            vm((W, W), BF),
            vm((W, W), BF),
            vm((W, W), BF),
            vm((4, 4, 2, SH, W), BF),
            vm((4, 4, 2, SH, W), BF),
            vm((4, 7, SH, W), BF),
            vm((4, 2, 4, SH, W), BF),
            vm((4, 7, SH, W), BF),
            vm((2, 8, SH, W), BF),
            vm((2, SH, 128), F32),
            vm((4, 2, SH, 128), BF),
            vm((2, 4, SH, 128), BF),
            vm((1, 7, SH, 128), BF),
            vm((2, SH, W), F32),
            vm((2, 4, SH, 128), BF),
            vm((4, SH, 128), BF),
            vm((1, 7, SH, 128), BF),
            vm((SH, W), F32),
            pltpu.SemaphoreType.DMA((n_send,)),
            pltpu.SemaphoreType.DMA((n_recv,)),
            pltpu.SemaphoreType.DMA((16,)),
            pltpu.SemaphoreType.DMA((4,)),
        ],
        compiler_params=pltpu.CompilerParams(
            collective_id=0, has_side_effects=True, vmem_limit_bytes=56 * 2**20
        ),
        name="memory_backward",
    )(
        query.reshape(shared), key.reshape(shared), value.reshape(shared), out_grad.reshape(shared), rate,
        memory_init, memory_cot,
    )
    return publish(*outs)


def publish_kernel(*refs):
    ins, outs, held, wide, (rsem, wsem) = refs[:4], refs[4:8], refs[8:12], refs[12], refs[13:]
    rows = [pl.ds(g * 128, 128) for g in range(8)]
    reads = [(ins[3].at[r], held[3].at[r]) for r in rows] + [(ins[i], held[i]) for i in range(3)]
    writes = [(wide.at[r], outs[3].at[r]) for r in rows] + [(held[i], outs[i]) for i in range(3)]
    reads = [pltpu.make_async_copy(*pair, rsem.at[i]) for i, pair in enumerate(reads)]
    writes = [pltpu.make_async_copy(*pair, wsem.at[i]) for i, pair in enumerate(writes)]
    for read in reads:
        read.start()
    for i, (read, write) in enumerate(zip(reads, writes)):
        read.wait()
        if i < 8:
            wide[rows[i], :] = held[3][rows[i], :].astype(F32)
        write.start()
    for write in writes:
        write.wait()


def publish(*arrays):
    shapes = [jax.ShapeDtypeStruct(a.shape, a.dtype) for a in arrays[:3]] + [jax.ShapeDtypeStruct((W, W), F32)]
    return pl.pallas_call(
        publish_kernel,
        out_shape=tuple(shapes),
        in_specs=[pl.BlockSpec(memory_space=pl.ANY)] * 4,
        out_specs=(pl.BlockSpec(memory_space=pl.ANY),) * 4,
        scratch_shapes=[pltpu.VMEM(a.shape, a.dtype) for a in arrays]
        + [pltpu.VMEM((W, W), F32), pltpu.SemaphoreType.DMA((11,)), pltpu.SemaphoreType.DMA((11,))],
        compiler_params=pltpu.CompilerParams(vmem_limit_bytes=60 * 2**20),
        name="publish",
    )(*arrays)


def solution(mesh):
    placed = (
        P("dp", None, None, "col"),
        P("dp", None, None, "col"),
        P("dp", None, None, "row"),
        P("dp", None, None, "row"),
        P("dp", None, None),
        P("row", "col"),
        P("row", "col"),
    )
    return jax.shard_map(
        on_device,
        mesh=mesh,
        in_specs=placed,
        out_specs=(
            P("dp", None, "row", "col"),
            P("dp", None, "row", "col"),
            P("dp", None, "col", "row"),
            P("row", "col"),
        ),
        check_vma=False,
    )
```

```python
import functools

import jax
import jax.numpy as jnp
from jax import lax
from jax.experimental import pallas as pl
from jax.experimental.pallas import tpu as pltpu
from jax.sharding import PartitionSpec as P

MESH = pl.DeviceIdType.MESH
BF, F32 = jnp.bfloat16, jnp.float32
W = 1024
SH = 64
NJ = 4
NQ = 2
CW, RW = W // NJ, SH // NJ
ALL = slice(0, W)
X_FIRST = frozenset([(0, 0), (0, 3), (1, 0), (1, 1), (1, 2), (2, 3)])
ROW_X_FIRST = frozenset([(2, 3), (3, 3)])
UNIT_US = 23.4
HOP_US = {"z+": 2.7, "z-": 2.7, "y+": 2.7, "y-": 2.7, "x": 3.7, "dp": 1.1}
CORE = 1.0
NT = (((1,), (1,)), ((), ()))
TN = (((0,), (0,)), ((), ()))
ORDER = (
    15, 7, 68, 23, 31, 63, 39, 47, 55, 104, 174, 69, 166, 64, 79, 0, 8, 16, 84, 56, 24, 74, 134, 1,
    9, 32, 118, 17, 142, 25, 40, 126, 96, 57, 33, 2, 48, 127, 26, 92, 18, 65, 41, 10, 34, 49, 3, 111,
    4, 28, 135, 100, 27, 19, 42, 11, 58, 36, 50, 35, 12, 66, 119, 128, 20, 21, 29, 5, 112, 44, 13, 43,
    159, 158, 37, 120, 136, 51, 52, 150, 22, 67, 167, 80, 45, 6, 30, 85, 82, 14, 75, 59, 70, 129, 87, 60,
    151, 97, 113, 53, 160, 38, 143, 168, 71, 61, 73, 137, 72, 101, 152, 130, 46, 121, 114, 210, 76, 144, 93, 131,
    54, 81, 62, 86, 161, 169, 139, 108, 132, 89, 83, 138, 115, 78, 153, 122, 116, 145, 98, 77, 102, 123, 133, 162,
    163, 88, 170, 194, 105, 171, 124, 140, 154, 117, 178, 155, 94, 146, 207, 164, 172, 147, 191, 90, 125, 186, 106, 156,
    141, 202, 175, 148, 165, 198, 208, 103, 95, 173, 206, 183, 157, 190, 149, 182, 107, 209, 211, 213, 195, 215, 187, 176,
    212, 109, 179, 184, 99, 192, 199, 203, 196, 188, 180, 200, 217, 204, 177, 216, 185, 189, 214, 218, 110, 91, 197, 201,
    193, 205, 181,
)


class Task:
    def __init__(self, name, needs, groups, waits, cost, body, starts, rank):
        self.name, self.needs, self.groups, self.waits, self.cost = name, needs, groups, waits, cost
        self.body, self.starts, self.rank = body, starts, rank


def order_tasks(tasks, links, sizes):
    free, arrive, done, now = {}, {}, {}, 0.0
    left, result = list(tasks), []
    while left:
        best = None
        for task in left:
            if any(n not in done for n in task.needs) or any(w not in arrive for w in task.waits):
                continue
            ready = max([now] + [done[n] for n in task.needs] + [arrive[w] for w in task.waits])
            key = (ready, task.rank)
            if best is None or key < best[0]:
                best = (key, task)
        (ready, _), task = best
        now = ready + CORE * task.cost + 0.03 * len(task.starts)
        done[task.name] = now
        for copy in task.starts:
            link = links[copy]
            begin = max(now, free.get(link, 0.0))
            free[link] = begin + sizes[copy]
            arrive[copy] = free[link] + HOP_US[link]
        left.remove(task)
        result.append(task)
    return result, now


def kernel(
    q_hbm, k_hbm, v_hbm, y_hbm, r_hbm, m_hbm, c_hbm,
    qg_hbm, kg_hbm, vg_hbm, ig_hbm,
    qg_ref, kg_ref, vg_ref, cf, kb, qb, yb, vb, rb, mf, mh0, mh1, ch, ph0, part, full, rbuf, part2, rbuf2, arec, rc, gpart, gfull, gbuf, fix, upart, ufull, ubuf, q1,
    ssem, rsem, lsem, osem,
):
    dp, row, col = lax.axis_index("dp"), lax.axis_index("row"), lax.axis_index("col")
    z, xh = col // 2, col % 2
    xl, y = row // 4, row % 4
    zp, zm, z2, xo = (z + 1) % 4, (z + 3) % 4, (z + 2) % 4, 1 - xh
    yp, ym, y2, lo = (y + 1) % 4, (y + 3) % 4, (y + 2) % 4, 1 - xl
    device = {
        "z+": (dp, row, zp * 2 + xh),
        "z-": (dp, row, zm * 2 + xh),
        "xh": (dp, row, z * 2 + xo),
        "y+": (dp, xl * 4 + yp, col),
        "y-": (dp, xl * 4 + ym, col),
        "xl": (dp, lo * 4 + y, col),
        "y2": (dp, xl * 4 + y2, col),
        "z2": (dp, row, z2 * 2 + xh),
        "dp": (1 - dp, row, col),
    }

    barrier = pltpu.get_barrier_semaphore()
    for partner in device.values():
        pl.semaphore_signal(barrier, inc=1, device_id=partner, device_id_type=MESH)

    loads = {}

    def load(name, src, dst):
        loads[name] = pltpu.make_async_copy(src, dst, lsem.at[len(loads)])

    def rows_of(g):
        return pl.ds(g * CW, CW)

    load("K1", k_hbm.at[0, 1], kb.at[1])
    for g in range(NJ):
        load(("C", g), c_hbm.at[rows_of(g)], cf.at[rows_of(g)])
    load("K0", k_hbm.at[0, 0], kb.at[0])
    for g in range(NJ):
        load(("M", g), m_hbm.at[rows_of(g)], mf.at[rows_of(g)])
    load("Y1", y_hbm.at[0, 1], yb.at[1])
    load("Q1", q_hbm.at[0, 1], qb.at[1])
    load("R", r_hbm, rb)
    load("V", v_hbm.at[0, :, col], vb)
    load("Y0", y_hbm.at[0, 0], yb.at[0])
    load("Q0", q_hbm.at[0, 0], qb.at[0])
    loaded = set()
    stages = [
        ["K1"] + [("C", g) for g in range(NJ)],
        ["K0"] + [("M", g) for g in range(NJ)],
        ["Y1", "Q1", "R", "V", "Y0", "Q0"],
    ]

    def next_stage():
        for name in stages.pop(0):
            loads[name].start()

    def need(*names):
        for name in names:
            if name in loaded:
                continue
            while any(name in stage for stage in stages):
                next_stage()
            loads[name].wait()
            loaded.add(name)
            if stages and name in (("C", 0), ("M", 0)):
                next_stage()

    next_stage()

    def rates():
        need("R")
        at = lax.broadcasted_iota(jnp.int32, (SH, 8 * SH), 1)
        own = lax.broadcasted_iota(jnp.int32, (SH, 8 * SH), 0) + col * SH
        for b in range(2):
            picked = jnp.where(at == own, jnp.broadcast_to(rb[0, b : b + 1, :], (SH, 8 * SH)), 0.0)
            rc[b] = jnp.broadcast_to(jnp.sum(picked, axis=1, keepdims=True), (SH, 128))

    copies, links, sizes, groups, sends = {}, {}, {}, {}, {}

    def waiter(ref, sem):
        return pltpu.make_async_copy(ref, ref, sem)

    def send_group(key, ref):
        sends[key] = waiter(ref, ssem.at[len(sends)]), ssem.at[len(sends)]

    def group(name, ref):
        groups[name] = waiter(ref, rsem.at[len(groups)]), rsem.at[len(groups)]

    def copy(name, link, src, dst, units, job, into=None, over=None):
        if into is None:
            group(name, dst)
            into = name
        copies[name] = pltpu.make_async_remote_copy(
            src_ref=src, dst_ref=dst, send_sem=sends[job][1], recv_sem=groups[into][1],
            device_id=device[link], device_id_type=MESH,
        )
        members.setdefault(into, []).append(name)
        links[name] = over or ("x" if link in ("xh", "xl") else link)
        sizes[name] = units * (UNIT_US if link != "dp" else 1.2)

    members = {}

    tasks = []

    def task(name, needs, waits, cost, body, starts, rank):
        tasks.append(Task(name, needs, waits, [c for w in waits for c in members[w]], cost, body, starts, rank))

    def out(i, ref, hbm, *index):
        pltpu.make_async_copy(ref.at[index], hbm.at[index], osem.at[i]).start()

    def f32(ref, *index):
        return ref[index].astype(F32)

    def finish(q, cs, rs, total):
        if "V" not in loaded:
            rates()
        need("V")
        b = 1 if q in (0, 3) else 0
        rate = jnp.broadcast_to(rc[b, rs, 0:1], total.shape)
        if q == 2:
            total = total + fix[0, rs, cs]
        if q == 3:
            total = 0.999 * total - fix[1, rs, cs]
        if q in (0, 2):
            scaled = (rate * total).astype(BF)
            vg_ref[0, b, rs, cs] = scaled
            out(2, vg_ref, vg_hbm, 0, b, rs, cs)
            full[q, z, xh, rs, cs] = -scaled
        else:
            full[q, z, xh, rs, cs] = (rate * (total - f32(vb, b, rs, cs))).astype(BF)

    def reduce_job(tag, q, rs, cs, rank, P4, R, first, pieces, names, after, after_cost, after_starts, more=()):
        ring, ahead, behind, far, mine, other = pieces
        up, down, side = names
        u = (rs.stop - rs.start) * (cs.stop - cs.start) / (SH * W) / 8.0

        def part_at(i, half):
            return P4(i, half)

        def slot(k):
            return R.at[q, k, rs, cs]

        n = lambda k: (tag, q, rank, k)
        job = (tag[0], q)
        if job not in sends:
            send_group(job, R.at[q])
        group(n("D1"), R.at[q, pl.ds(0, 2), rs, cs])
        group(n("A"), R.at[q, pl.ds(0, 3), rs, cs])
        group(n("B"), R.at[q, pl.ds(0, 2), rs, cs])
        copy(n("D1p"), up, part_at(far, mine), slot(0), u, job, n("D1"))
        copy(n("D1m"), down, part_at(far, other), slot(1), u, job, n("D1"))
        copy(n("D2pA"), up, part_at(ahead, mine), slot(2), u, job, n("A"))
        copy(n("D2pB"), up, part_at(ahead, other), slot(3), u, job, n("B"))
        copy(n("D2mA"), down, part_at(behind, mine), slot(4), u, job, n("A"))
        copy(n("D2mB"), down, part_at(behind, other), slot(5), u, job, n("B"))
        copy(n("DX"), side, part_at(ring, other), slot(6), u, job, n("A"))

        def add(ref, *slots):
            total = ref[...].astype(F32)
            for k in slots:
                total = total + R[q, k, rs, cs].astype(F32)
            return total

        def s1():
            ref = part_at(ahead, mine)
            ref[...] = add(ref, 0).astype(BF)
            ref = part_at(behind, other)
            ref[...] = add(ref, 1).astype(BF)

        def s2():
            ref = part_at(ring, other)
            ref[...] = add(ref, 3, 5).astype(BF)

        def s3():
            after(rs, cs, add(part_at(ring, mine), 2, 4, 6))

        vpu = u * 8 * 0.1 + 0.03
        task(n("s1"), [first], [n("D1")], 2 * vpu, s1, [n("D2pA"), n("D2mB")], rank)
        task(n("s2"), [n("s1")], [n("B")], vpu, s2, [n("DX")], rank)
        task(n("s3"), [n("s2")], [n("A")], vpu + after_cost, s3, after_starts, rank)
        tasks[-1].needs.extend(more)
        return [n("D1p"), n("D1m"), n("D2pB"), n("D2mA")], n("s3")

    def gather_job(tag, q, rs, cs, rank, F4, R, pieces, names):
        ring, ahead, behind, _, mine, other = pieces
        up, down, side = names
        u = (rs.stop - rs.start) * (cs.stop - cs.start) / (SH * W) / 8.0
        n = lambda k: (tag, q, rank, k)
        job = (tag[0], q)
        group(n("G"), R.at[q, pl.ds(0, 4), rs, cs])
        copy(n("GX"), side, F4(ring, mine), F4(ring, mine), u, job)
        copy(n("Gop"), up, F4(ring, mine), F4(ring, mine), u, job)
        copy(n("Gom"), down, F4(ring, mine), F4(ring, mine), u, job, n("G"))
        copy(n("Gtp"), up, F4(ring, other), F4(ring, other), u, job, n("G"))
        copy(n("Gtm"), down, F4(ring, other), F4(ring, other), u, job)
        copy(n("Fp"), up, F4(behind, mine), F4(behind, mine), u, job, n("G"))
        copy(n("Fm"), down, F4(ahead, other), F4(ahead, other), u, job, n("G"))

        def follow(last):
            task(n("s4"), [last], [n("GX")], 0.05, None, [n("Gtp"), n("Gtm")], rank)
            task(n("s5p"), [last], [n("Gop")], 0.05, None, [n("Fp")], rank)
            task(n("s5m"), [last], [n("Gtm")], 0.05, None, [n("Fm")], rank)
            task(n("end"), [n("s4"), n("s5p"), n("s5m")], [n("G")], 0.05, None, [], rank)
            return n("end")

        return [n("GX"), n("Gop"), n("Gom")], follow

    z_ring, z_names = (z, zp, zm, z2, xh, xo), ("z+", "z-", "xh")
    y_ring, y_names = (y, yp, ym, y2, xl, lo), ("y+", "y-", "xl")

    def col_sends(q):
        if ("c", q) not in sends:
            send_group(("c", q), rbuf.at[pl.ds(0, 2)])

    def col_z(q, rs, cs, rank, first, more):
        def P4(i, half):
            return part.at[q, i, half, rs, cs]

        def F4(i, half):
            return full.at[q, i, half, rs, cs]

        col_sends(q)
        begin, follow = gather_job("cz", q, rs, cs, rank, F4, rbuf, z_ring, z_names)
        starts, last = reduce_job(
            "cz", q, rs, cs, rank, P4, rbuf, first, z_ring, z_names,
            lambda rs, cs, total: finish(q, cs, rs, total), 0.1, begin, more,
        )
        return starts, follow(last)

    def keys_job(rank, first):
        rs, cs = slice(0, SH), slice(0, 128)

        n = lambda k: ("kk", 0, rank, k)
        u, job = 1 / 64, ("k", 0)
        send_group(job, rbuf.at[pl.ds(0, 2), :, rs, cs])
        group(n("Z"), gbuf.at[0, pl.ds(0, 6)])
        group(n("Y"), gbuf.at[0, pl.ds(0, 6)])
        for i, (there, at, cost) in enumerate((("z+", zp, 1), ("z-", zm, 1), ("z2", z2, 2))):
            over = "z+" if i == 2 else there
            copy(n(there), there, gpart.at[at], gbuf.at[0, pl.ds(2 * i, 2)], 2 * cost * u, job, n("Z"), over)
        copy(n("DX"), "xh", gpart.at[z, xo], gbuf.at[0, 6], u, job)
        copy(n("GX"), "xl", gfull.at[xl, y], gfull.at[xl, y], u, job)
        for there, cost in (("y+", 1), ("y-", 1), ("y2", 2)):
            over = "y+" if there == "y2" else there
            copy(n(there), there, gfull.at[:, y], gfull.at[:, y], 2 * cost * u, job, n("Y"), over)

        def s1():
            for half in (xo, xh):
                total = gpart[z, half].astype(F32)
                for i in range(3):
                    total = total + gbuf[0, 2 * i + half].astype(F32)
                gpart[z, half] = total.astype(BF)

        def s2():
            gfull[xl, y] = (gpart[z, xh].astype(F32) + gbuf[0, 6].astype(F32)).astype(BF)

        task(n("s1"), [first], [n("Z")], 0.1, s1, [n("DX")], rank)
        task(n("s2"), [n("s1")], [n("DX")], 0.06, s2, [n("GX")], rank)
        task(n("s3"), [n("s2")], [n("GX")], 0.06, None, [n("y+"), n("y-"), n("y2")], rank)
        task(n("end"), [n("s3")], [n("Y")], 0.06, None, [], rank)
        return [n("z+"), n("z-"), n("z2")], n("end")

    def col_x(q, rs, cs, rank, first, more):
        u = (rs.stop - rs.start) * (cs.stop - cs.start) / (SH * W) / 8.0
        half = (cs.stop - cs.start) // 2
        cl, cr = slice(cs.start, cs.start + half), slice(cs.start + half, cs.stop)
        n = lambda k: ("cx", q, rank, k)

        def P3(i, c):
            return part.at[q, i, xh, rs, c]

        def F3(i, c):
            return full.at[q, i, xh, rs, c]

        def slot(k, c):
            return rbuf.at[q, k, rs, c]

        job = ("c", q)
        col_sends(q)
        group(n("D1"), slot(4, cs))
        group(n("D2"), rbuf.at[q, pl.ds(0, 2), rs, cs])
        group(n("F"), slot(4, cs))
        group(n("X"), rbuf.at[q, pl.ds(0, 4), rs, cs])
        copy(n("DX"), "xh", part.at[q, :, xo, rs, cs], rbuf.at[q, pl.ds(0, 4), rs, cs], 4 * u, job)
        copy(n("D1p"), "z+", P3(z2, cl), slot(4, cl), u / 2, job, n("D1"))
        copy(n("D1m"), "z-", P3(z2, cr), slot(4, cr), u / 2, job, n("D1"))
        copy(n("D2pL"), "z+", P3(zp, cl), slot(5, cl), u / 2, job, n("D2"))
        copy(n("D2pR"), "z+", P3(zp, cr), slot(5, cr), u / 2, job, n("D2"))
        copy(n("D2mL"), "z-", P3(zm, cl), slot(6, cl), u / 2, job, n("D2"))
        copy(n("D2mR"), "z-", P3(zm, cr), slot(6, cr), u / 2, job, n("D2"))
        copy(n("Gp"), "z+", F3(z, cs), F3(z, cs), u, job)
        copy(n("Gm"), "z-", F3(z, cs), F3(z, cs), u, job)
        copy(n("Fp"), "z+", F3(zm, cl), F3(zm, cl), u / 2, job, n("F"))
        copy(n("Fm"), "z-", F3(zp, cr), F3(zp, cr), u / 2, job, n("F"))
        copy(n("X0"), "xh", F3(z, cs), F3(z, cs), u, job, n("X"))
        copy(n("Xm"), "xh", F3(zm, cs), F3(zm, cs), u, job, n("X"))
        copy(n("Xp"), "xh", F3(zp, cs), F3(zp, cs), u, job, n("X"))
        copy(n("X2"), "xh", F3(z2, cs), F3(z2, cs), u, job, n("X"))

        def s1():
            for i in range(4):
                part[q, i, xh, rs, cs] = (f32(part, q, i, xh, rs, cs) + f32(rbuf, q, i, rs, cs)).astype(BF)

        def s2():
            part[q, zp, xh, rs, cl] = (f32(part, q, zp, xh, rs, cl) + f32(rbuf, q, 4, rs, cl)).astype(BF)
            part[q, zm, xh, rs, cr] = (f32(part, q, zm, xh, rs, cr) + f32(rbuf, q, 4, rs, cr)).astype(BF)

        def s3():
            finish(q, cs, rs, f32(part, q, z, xh, rs, cs) + f32(rbuf, q, 5, rs, cs) + f32(rbuf, q, 6, rs, cs))

        vpu = u * 8 * 0.1 + 0.03
        task(n("s1"), [first], [n("DX")], 2 * vpu, s1, [n("D1p"), n("D1m"), n("D2pR"), n("D2mL")], rank)
        task(n("s2"), [n("s1")], [n("D1")], 2 * vpu, s2, [n("D2pL"), n("D2mR")], rank)
        task(n("s3"), [n("s2"), *more], [n("D2")], vpu + 0.1, s3, [n("Gp"), n("Gm"), n("X0")], rank)
        task(n("s4p"), [n("s3")], [n("Gp")], 0.05, None, [n("Fp"), n("Xm")], rank)
        task(n("s4m"), [n("s3")], [n("Gm")], 0.05, None, [n("Fm"), n("Xp")], rank)
        task(n("s5"), [n("s4p"), n("s4m")], [n("F")], 0.05, None, [n("X2")], rank)
        task(n("end"), [n("s5")], [n("X")], 0.05, None, [], rank)
        return [n("DX")], n("end")

    def row_job(u, rs, cs, rank, first):
        def P4(i, half):
            return part2.at[u, half, i, rs, cs]

        def store(rs, cs, total):
            if u == 1:
                q1[rs, cs] = total
                return
            i, b = u // 2, u % 2
            ref, hbm = ((qg_ref, qg_hbm), (kg_ref, kg_hbm))[i]
            ref[0, b, rs, cs] = total.astype(BF)
            out(i, ref, hbm, 0, b, rs, cs)

        return reduce_job(
            "r", u, rs, cs, rank, P4, rbuf2, first, y_ring, y_names, store, 0.0, [],
        )

    def row_x(u, rs, cs, rank, first):
        share = (rs.stop - rs.start) * (cs.stop - cs.start) / (SH * W) / 8.0
        half = (cs.stop - cs.start) // 2
        cl, cr = slice(cs.start, cs.start + half), slice(cs.start + half, cs.stop)
        n = lambda k: ("rx", u, rank, k)
        job = ("r", u)
        if job not in sends:
            send_group(job, rbuf2.at[u])
        P3 = lambda i, c: part2.at[u, xl, i, rs, c]
        slot = lambda k, c: rbuf2.at[u, k, rs, c]
        group(n("D1"), slot(4, cs))
        group(n("D2"), rbuf2.at[u, pl.ds(0, 2), rs, cs])
        copy(n("DX"), "xl", part2.at[u, lo, :, rs, cs], rbuf2.at[u, pl.ds(0, 4), rs, cs], 4 * share, job)
        copy(n("D1p"), "y+", P3(y2, cl), slot(4, cl), share / 2, job, n("D1"))
        copy(n("D1m"), "y-", P3(y2, cr), slot(4, cr), share / 2, job, n("D1"))
        copy(n("D2pL"), "y+", P3(yp, cl), slot(5, cl), share / 2, job, n("D2"))
        copy(n("D2pR"), "y+", P3(yp, cr), slot(5, cr), share / 2, job, n("D2"))
        copy(n("D2mL"), "y-", P3(ym, cl), slot(6, cl), share / 2, job, n("D2"))
        copy(n("D2mR"), "y-", P3(ym, cr), slot(6, cr), share / 2, job, n("D2"))

        def s1():
            for i in range(4):
                part2[u, xl, i, rs, cs] = (f32(part2, u, xl, i, rs, cs) + f32(rbuf2, u, i, rs, cs)).astype(BF)

        def s2():
            part2[u, xl, yp, rs, cl] = (f32(part2, u, xl, yp, rs, cl) + f32(rbuf2, u, 4, rs, cl)).astype(BF)
            part2[u, xl, ym, rs, cr] = (f32(part2, u, xl, ym, rs, cr) + f32(rbuf2, u, 4, rs, cr)).astype(BF)

        def s3():
            total = f32(part2, u, xl, y, rs, cs) + f32(rbuf2, u, 5, rs, cs) + f32(rbuf2, u, 6, rs, cs)
            kg_ref[0, u - 2, rs, cs] = total.astype(BF)
            out(1, kg_ref, kg_hbm, 0, u - 2, rs, cs)

        task(n("s1"), [first], [n("DX")], 0.1, s1, [n("D1p"), n("D1m"), n("D2pR"), n("D2mL")], rank)
        task(n("s2"), [n("s1")], [n("D1")], 0.06, s2, [n("D2pL"), n("D2mR")], rank)
        task(n("s3"), [n("s2")], [n("D2")], 0.06, s3, [], rank)
        return [n("DX")], n("s3")

    def dot(a, b, dims=None):
        if dims is None:
            return jnp.dot(a, b, preferred_element_type=F32)
        return lax.dot_general(a, b, dims, preferred_element_type=F32)

    def whole(ref, *index):
        return ref[index].reshape(8 * SH, -1)

    def some(ref, *index):
        return ref[index].reshape(8 * RW, W)

    ends = [[None] * NJ for _ in range(4)]
    everything = slice(0, SH)
    full_cols = slice(0, W)

    def cols(g):
        return slice(g * CW, (g + 1) * CW)

    def toks(k):
        return slice(k * RW, (k + 1) * RW)

    def spread(q, block, width, value, rs, cs):
        part[q, :, :, rs, cs] = value.astype(BF).reshape(4, 2, rs.stop - rs.start, cs.stop - cs.start)

    def phase_a(q, g, rank):
        b, src, half = (1, cf, ch) if q == 0 else (0, mf, mh0)
        rs, cs = everything, cols(g)
        name = ("P", q, g)

        def body():
            need("K1" if q == 0 else "K0", ("C" if q == 0 else "M", g))
            half[cs, :] = src[cs, :].astype(BF)
            spread(q, g, CW, dot(whole(kb, b), half[cs, :], NT), rs, cs)

        make = col_x if (q, g) in X_FIRST else col_z
        starts, ends[q][g] = make(q, rs, cs, rank, name, [])
        task(name, [], [], 0.35, body, starts, rank)

    for i, (q, g) in enumerate([(0, g) for g in range(NJ)] + [(1, g) for g in range(NJ)]):
        phase_a(q, g, i)

    def keys_product():
        name = ("KK",)

        def body():
            need("K0", "K1")
            odd = y % 2
            rhs = kb[odd, pl.ds(2 * (row // 2), 2)].reshape(128, W)
            value = dot(kb[1 - odd].reshape(8 * SH, W), rhs, NT)
            gpart[...] = value.astype(BF).reshape(4, 2, SH, 128)

        starts, end = keys_job(7.2, name)
        task(name, [], [], 0.4, body, starts, 7.2)
        return end

    keys_end = keys_product()

    def correction(q, g):
        cs = cols(g)
        src, odd = (0, 1) if q == 2 else (1, 0)

        def body():
            lhs = jnp.concatenate([gfull[r // 4, r % 4] for r in range(odd, 8, 2)], axis=1)
            fix[q - 2, :, cs] = dot(lhs, full[src, :, :, :, cs].reshape(8 * SH, CW))

        task(("FX", q, g), [keys_end, ends[src][g]], [], 0.08, body, [], 7.4 if q == 2 else 8.4)

    def project_known(g):
        cs = cols(g)

        def body():
            need("Y1", "Q1")
            step = dot(yb[1, :, :, cs].reshape(8 * SH, CW), whole(qb, 1), TN)
            before = cf[cs, :]
            cf[cs, :] = 0.999 * before + step
            ph0[cs, :] = (1.899 * before + step).astype(BF)

        task(("PK", g), [("P", 0, g)], [], 0.35, body, [], 7.1)

    def project_update(g):
        cs = cols(g)

        def body():
            step = dot(full[0, :, :, :, cs].reshape(8 * SH, CW), whole(kb, 1), TN)
            adjoint = cf[cs, :] + step
            cf[cs, :] = adjoint
            ph0[cs, :] = (adjoint + 0.9 * ch[cs, :].astype(F32)).astype(BF)

        task(("PU", g), [ends[0][g]] + [("P", 2, k) for k in range(NJ)], [], 0.45, body, [], 16.1)

    def memory_update(g):
        cs = cols(g)

        def body():
            need("K0")
            step = dot(full[1, :, :, :, cs].reshape(8 * SH, CW), whole(kb, 0), TN)
            mh1[cs, :] = (0.999 * mf[cs, :] - step).astype(BF)

        task(("MU", g), [ends[1][g]], [], 0.38, body, [], 16.2)

    for g in range(NJ):
        project_known(g)
        correction(2, g)
        correction(3, g)
        project_update(g)
        memory_update(g)
    all_pu = [("PU", g) for g in range(NJ)]
    all_mu = [("MU", g) for g in range(NJ)]

    def query_part(u, g, rank):
        rs, cs = everything, slice(g * W // NQ, (g + 1) * W // NQ)
        name = ("QP", u, g)

        def body():
            need("Y%d" % u)
            for lo in range(cs.start, cs.stop, CW):
                value = dot(whole(yb, u), mh0[:, lo : lo + CW])
                part2[u, :, :, rs, lo : lo + CW] = value.astype(BF).reshape(2, 4, SH, CW)

        starts, last = row_job(u, rs, cs, rank, name)
        task(name, [("P", 1, g) for g in range(NJ)], [], 0.6, body, starts, rank)

        return last

    for g in range(NQ):
        query_part(0, g, 20 + g)
    q1_sums = [query_part(1, g, 24 + g) for g in range(NQ)]

    def query_update():
        rank, rs, cs = 16.5, slice(0, SH), slice(0, 128)
        n = lambda k: ("u", 0, rank, k)

        def body():
            value = dot(whole(yb, 1), full[1, z].reshape(128, W), NT)
            upart[...] = value.astype(BF).reshape(2, 4, SH, 128)

        def store(rs, cs, total):
            ufull[z] = total.astype(BF)

        send_group(("u", 0), rbuf.at[pl.ds(0, 2), pl.ds(0, 5), rs, cs])
        copy(n("Gp"), "z+", ufull.at[z], ufull.at[z], 1 / 64, ("u", 0))
        group(n("G"), gbuf.at[0, pl.ds(0, 2)])
        copy(n("Gm"), "z-", ufull.at[z], ufull.at[z], 1 / 64, ("u", 0), n("G"))
        copy(n("F"), "z+", ufull.at[zm], ufull.at[zm], 1 / 64, ("u", 0), n("G"))
        starts, last = reduce_job(
            "u", 0, rs, cs, rank, lambda i, half: upart.at[half, i], ubuf, ("UP",), y_ring, y_names, store, 0.0,
            [n("Gp"), n("Gm")],
        )
        task(("UP",), ends[1], [], 0.3, body, starts, rank)
        task(n("s4"), [last], [n("Gp")], 0.05, None, [n("F")], rank)

        def final():
            lhs = jnp.concatenate([ufull[i] for i in range(4)], axis=1)
            for g in range(NJ):
                step = dot(lhs, kb[0, :, :, cols(g)].reshape(8 * SH, CW))
                qg_ref[0, 1, :, cols(g)] = (0.999 * q1[:, cols(g)] - step).astype(BF)
            out(0, qg_ref, qg_hbm, 0, 1)

        task(("QF",), [n("s4")] + q1_sums, [n("G")], 0.3, final, [], 32)

    query_update()

    def phase_b(q, k, rank):
        b, half = (0, ph0) if q == 2 else (1, mh0)
        deps = [("PK", g) if q == 2 else ("P", 1, g) for g in range(NJ)]
        rs, cs = toks(k), full_cols
        name = ("P", q, k)

        def body():
            need("K%d" % b)
            lhs = some(kb, b, slice(None), rs)
            for n in range(NJ):
                spread(q, n, CW, dot(lhs, half[cols(n), :], NT), rs, cols(n))

        make = col_x if (q, k) in X_FIRST else col_z
        starts, ends[q][k] = make(q, rs, cs, rank, name, [("FX", q, g) for g in range(NJ)])
        task(name, deps, [], 0.7, body, starts, rank)

    for i, (q, k) in enumerate([(2, k) for k in range(NJ)] + [(3, k) for k in range(NJ)]):
        phase_b(q, k, 8 + i)

    def key_part(u, k, rank):
        rs = toks(k)
        f, w, mem, proj = (2, 1, mh0, ph0) if u == 2 else (0, 3, mh1, ch)
        name = ("KP", u, k)

        def body():
            err, wgt = some(full, f, slice(None), slice(None), rs), some(full, w, slice(None), slice(None), rs)
            for n in range(NJ):
                value = dot(err, mem[:, cols(n)]) - dot(wgt, proj[:, cols(n)])
                part2[u, :, :, rs, cols(n)] = value.astype(BF).reshape(2, 4, RW, CW)

        starts, _ = (row_x if (u, k) in ROW_X_FIRST else row_job)(u, rs, full_cols, rank, name)
        deps = [ends[2][k]] + all_pu + all_mu if u == 2 else [ends[3][k]] + all_pu + all_mu
        task(name, deps, [], 0.65, body, starts, rank)

    for k in range(NJ):
        key_part(2, k, 17 + k / 10)
        key_part(3, k, 18 + k / 10)

    def adjoint_early(g):
        cs = cols(g)

        def body():
            need("Y0", "Q0")
            cf[cs, :] = 0.999 * cf[cs, :] + dot(yb[0, :, :, cs].reshape(8 * SH, CW), whole(qb, 0), TN)

        task(("AE", g), [("PU", g)], [], 0.38, body, [], 30)

    def adjoint_late(g):
        cs = cols(g)

        def body():
            step = dot(full[2, :, :, :, cs].reshape(8 * SH, CW), whole(kb, 0), TN)
            qb[g // 2, four] = (cf[cs, :] + step).astype(BF).reshape(4, SH, W)

        four = slice(g % 2 * 4, g % 2 * 4 + 4)
        copy(("A", g), "dp", qb.at[g // 2, four], arec.at[g // 2, four], 0.5, "A")
        task(("AL", g), [("AE", h) for h in range(NJ)] + ends[2], [], 0.38, body, [("A", g)], 19)

        def total():
            both = qb[g // 2, four].astype(F32) + arec[g // 2, four].astype(F32)
            ph0[cs, :] = both.astype(BF).reshape(CW, W)
            out(3, ph0, ig_hbm, cs)

        task(("AT", g), [("AL", g)] + [("KP", 2, k) for k in range(NJ)], [("A", g)], 0.1, total, [], 31)

    for g in range(NJ):
        adjoint_early(g)
    send_group("A", arec)
    for g in range(NJ):
        adjoint_late(g)

    order, _ = order_tasks(tasks, links, sizes)
    if ORDER:
        order = [tasks[i] for i in ORDER]
    held = []
    for item in order:
        if held is not None and (item.groups or len(held) == 2):
            pl.semaphore_wait(barrier, len(device))
            for name in [name for early in held for name in early.starts]:
                copies[name].start()
            held = None
        for name in item.groups:
            groups[name][0].wait()
        if item.body is not None:
            item.body()
        if held is not None:
            held.append(item)
            continue
        for name in item.starts:
            copies[name].start()
    for wait, _ in sends.values():
        wait.wait()
    for i, (ref, hbm) in enumerate(((qg_ref, qg_hbm), (kg_ref, kg_hbm), (vg_ref, vg_hbm), (ph0, ig_hbm))):
        pltpu.make_async_copy(ref, hbm, osem.at[i]).wait()


def on_device(query, key, value, out_grad, rate, memory_init, memory_cot):
    shared = (1, 2, 8, SH, W)
    vm = pltpu.VMEM
    n_recv, n_send = 16 * 7 + 4 + (2 * NQ + 8) * 3 + 5 + NJ, 11
    outs = pl.pallas_call(
        kernel,
        out_shape=(
            jax.ShapeDtypeStruct((1, 2, SH, W), BF),
            jax.ShapeDtypeStruct((1, 2, SH, W), BF),
            jax.ShapeDtypeStruct((1, 2, SH, W), BF),
            jax.ShapeDtypeStruct((W, W), BF),
        ),
        in_specs=[pl.BlockSpec(memory_space=pltpu.HBM)] * 7,
        out_specs=(pl.BlockSpec(memory_space=pl.ANY),) * 4,
        scratch_shapes=[
            vm((1, 2, SH, W), BF),
            vm((1, 2, SH, W), BF),
            vm((1, 2, SH, W), BF),
            vm((W, W), F32),
            vm((2, 8, SH, W), BF),
            vm((2, 8, SH, W), BF),
            vm((2, 8, SH, W), BF),
            vm((2, SH, W), BF),
            vm((1, 2, 8 * SH), F32),
            vm((W, W), F32),
            vm((W, W), BF),
            vm((W, W), BF),
            vm((W, W), BF),
            vm((W, W), BF),
            vm((4, 4, 2, SH, W), BF),
            vm((4, 4, 2, SH, W), BF),
            vm((4, 7, SH, W), BF),
            vm((4, 2, 4, SH, W), BF),
            vm((4, 7, SH, W), BF),
            vm((2, 8, SH, W), BF),
            vm((2, SH, 128), F32),
            vm((4, 2, SH, 128), BF),
            vm((2, 4, SH, 128), BF),
            vm((1, 7, SH, 128), BF),
            vm((2, SH, W), F32),
            vm((2, 4, SH, 128), BF),
            vm((4, SH, 128), BF),
            vm((1, 7, SH, 128), BF),
            vm((SH, W), F32),
            pltpu.SemaphoreType.DMA((n_send,)),
            pltpu.SemaphoreType.DMA((n_recv,)),
            pltpu.SemaphoreType.DMA((16,)),
            pltpu.SemaphoreType.DMA((4,)),
        ],
        compiler_params=pltpu.CompilerParams(
            collective_id=0, has_side_effects=True, vmem_limit_bytes=56 * 2**20
        ),
        name="memory_backward",
    )(
        query.reshape(shared), key.reshape(shared), value.reshape(shared), out_grad.reshape(shared), rate,
        memory_init, memory_cot,
    )
    return publish(*outs)


def publish_kernel(*refs):
    ins, outs, held, wide, (rsem, wsem) = refs[:4], refs[4:8], refs[8:12], refs[12], refs[13:]
    rows = [pl.ds(g * 128, 128) for g in range(8)]
    reads = [(ins[i], held[i]) for i in range(3)] + [(ins[3].at[r], held[3].at[r]) for r in rows]
    writes = [(held[i], outs[i]) for i in range(3)] + [(wide.at[r], outs[3].at[r]) for r in rows]
    reads = [pltpu.make_async_copy(*pair, rsem.at[i]) for i, pair in enumerate(reads)]
    writes = [pltpu.make_async_copy(*pair, wsem.at[i]) for i, pair in enumerate(writes)]
    for read in reads:
        read.start()
    for i, (read, write) in enumerate(zip(reads, writes)):
        read.wait()
        if i >= 3:
            wide[rows[i - 3], :] = held[3][rows[i - 3], :].astype(F32)
        write.start()
    for write in writes:
        write.wait()


def publish(*arrays):
    shapes = [jax.ShapeDtypeStruct(a.shape, a.dtype) for a in arrays[:3]] + [jax.ShapeDtypeStruct((W, W), F32)]
    return pl.pallas_call(
        publish_kernel,
        out_shape=tuple(shapes),
        in_specs=[pl.BlockSpec(memory_space=pl.ANY)] * 4,
        out_specs=(pl.BlockSpec(memory_space=pl.ANY),) * 4,
        scratch_shapes=[pltpu.VMEM(a.shape, a.dtype) for a in arrays]
        + [pltpu.VMEM((W, W), F32), pltpu.SemaphoreType.DMA((11,)), pltpu.SemaphoreType.DMA((11,))],
        compiler_params=pltpu.CompilerParams(vmem_limit_bytes=60 * 2**20),
        name="publish",
    )(*arrays)


def solution(mesh):
    placed = (
        P("dp", None, None, "col"),
        P("dp", None, None, "col"),
        P("dp", None, None, "row"),
        P("dp", None, None, "row"),
        P("dp", None, None),
        P("row", "col"),
        P("row", "col"),
    )
    return jax.shard_map(
        on_device,
        mesh=mesh,
        in_specs=placed,
        out_specs=(
            P("dp", None, "row", "col"),
            P("dp", None, "row", "col"),
            P("dp", None, "col", "row"),
            P("row", "col"),
        ),
        check_vma=False,
    )
```
